32 devices in a mesh: group: 2 (over y), node: 4 (over z), local: 4 (over x, core).
Axes of the slice: x: 2, y: 2, z: 4, core: 2. Of those that a mesh axis runs over, the one named last changes fastest.
Arguments:
- attended: bfloat16 [256, 5120], P(('group', 'node'), 'local'), parts along dimension 0, may hold values from -6 to 6
- norm_gain: float32 [5120], replicated, may hold values from 0.5 to 1.5
- node_ids: int32 [256, 2], P(('group', 'node', 'local')), parts along dimension 0, may hold values from 0 to 3, as said below
- gates: bfloat16 [256, 2, 2], P(('group', 'node', 'local')), parts along dimension 0, may hold values from 0.099609375 to 0.796875
- w_gate: bfloat16 [8, 5120, 2048], P('node', None, 'local'), may hold values from -0.078125 to 0.078125
- w_up: bfloat16 [8, 5120, 2048], P('node', None, 'local'), may hold values from -0.078125 to 0.078125
- w_down: bfloat16 [8, 2048, 5120], P('node', 'local'), may hold values from -0.25 to 0.25
- s_gate: bfloat16 [5120, 1024], P(None, 'local'), may hold values from -0.078125 to 0.078125
- s_up: bfloat16 [5120, 1024], P(None, 'local'), may hold values from -0.078125 to 0.078125
- s_down: bfloat16 [1024, 5120], P('local'), may hold values from -0.375 to 0.375
Outputs:
- mixed: bfloat16 [256, 5120], P(('group', 'node', 'local')), parts along dimension 0
The draws below stay inside these ranges and needn't reach their ends.
There are 2 independent parts, one for each index of `group`. The reference program is written for one: setup_inputs(seed, part) draws one part's arguments, and reference() takes and returns one part's arrays. A program takes and returns all parts, laid end to end along the dimension named above; an argument that names none is the same for every part. Nothing has to cross between parts.
Inputs may be any that keep to these rules, and one draw needn't show every extreme that they name: `node_ids`: each token's 2 node ids are distinct. Among the 8 tokens of one device no node is named by more than 6 tokens, and in every draw some node is named by exactly 6 tokens of every device.
All inputs are finite; a program needn't handle non-finite values.
Results may differ from the reference program's by a relative error of at most 0.0085.
Values may be sent and summed in bfloat16 or wider, within the bound.
No kernel may reach another device: no remote copies, remote signals or barrier semaphores. Data moves between devices by JAX's collectives and lax.ppermute only.
A program may use at most 128 MiB of HBM per device.

```python
import math
import jax
import jax.numpy as jnp
from jax import lax

D = 5120
FF_WIN = 2048
SH_WIN = 1024
EXP_NODE = 2
TOK_DEV = 8
PICK = 2
CAP = 6
EXPERTS = 8
TOKENS = 128
N_NODE = 4
N_LOCAL = 4


def draw_node_ids(key, part):
    key = jax.random.fold_in(key, 11)
    key_order, key_offset, key_ranks = jax.random.split(key, 3)
    devices_part = N_NODE * N_LOCAL
    order = jax.random.permutation(key_order, N_NODE).astype(jnp.int32)
    offsets = jax.random.randint(key_offset, (devices_part, 1, 1), 0, N_NODE - 1).astype(jnp.int32)
    rank_keys = jax.random.split(key_ranks, devices_part)
    ranks = jax.vmap(lambda sub: jax.random.permutation(sub, TOK_DEV))(rank_keys).astype(jnp.int32)
    is_hot = (ranks < CAP).astype(jnp.int32)
    before = ranks * PICK - jnp.minimum(ranks, CAP)
    picks = jnp.arange(PICK, dtype=jnp.int32)
    counter = before[:, :, None] + picks[None, None, :] - is_hot[:, :, None]
    cycled = (counter + offsets) % (N_NODE - 1)
    others = order[1 + cycled]
    hot_slot = is_hot[:, :, None] * (picks[None, None, :] == 0).astype(jnp.int32) > 0
    chosen = jnp.where(hot_slot, order[0], others)
    return chosen.reshape(devices_part * TOK_DEV, PICK).astype(jnp.int32)


def block_levels(key, shape, shards, smallest, largest):
    level = 1.0
    for position, parts in shards:
        heights = jax.random.uniform(jax.random.fold_in(jax.random.fold_in(key, 6), position), (parts,), jnp.float32, smallest / len(shards), largest / len(shards))
        level = level * jnp.repeat(jnp.exp(heights), shape[position] // parts).reshape((-1,) + (1,) * (len(shape) - 1 - position))
    return level


def noise(stream_key, shape, deviation, bound, pieces=(), kind=jnp.bfloat16):
    entries = deviation * jax.random.normal(stream_key, shape, jnp.float32)
    if pieces:
        entries = entries * block_levels(stream_key, shape, pieces, -0.22, 0.18)
    return jnp.clip(entries, -bound, bound).astype(kind)


def setup_inputs(seed: int = 0, part: int = 0) -> dict:
    key_list = jax.random.split(jax.random.key(seed), 11)
    part_splits = jax.random.split(jax.random.fold_in(key_list[10], part), 11)
    attended = noise(part_splits[0], (TOKENS, D), 1.0, 6.0, ((0, 4), (1, 4)))
    norm_gain = jnp.clip(1.0 + 0.1 * jax.random.normal(key_list[1], (D,), jnp.float32), 0.5, 1.5)
    node_ids = draw_node_ids(jax.random.fold_in(jax.random.fold_in(key_list[10], part), 71), part)
    gates = jnp.clip(jnp.exp(math.log(0.796875) - 2.0794415 * jax.random.uniform(part_splits[3], (TOKENS, PICK, EXP_NODE), jnp.float32) ** block_levels(part_splits[3], (TOKENS, PICK, EXP_NODE), ((0, 16),), -0.2, 0.2)), 0.099609375, 0.796875).astype(jnp.bfloat16)
    w_gate = noise(key_list[4], (EXPERTS, D, FF_WIN), D ** -0.5, 0.078125, ((0, 4), (2, 4)))
    w_up = noise(key_list[5], (EXPERTS, D, FF_WIN), D ** -0.5, 0.078125, ((0, 4), (2, 4)))
    w_down = noise(key_list[6], (EXPERTS, FF_WIN, D), (FF_WIN // 4) ** -0.5, 0.25, ((0, 4), (1, 4)))
    s_gate = noise(key_list[7], (D, SH_WIN), D ** -0.5, 0.078125, ((1, 4),))
    s_up = noise(key_list[8], (D, SH_WIN), D ** -0.5, 0.078125, ((1, 4),))
    s_down = noise(key_list[9], (SH_WIN, D), (SH_WIN // 4) ** -0.5, 0.375, ((0, 4),))
    return dict(attended=attended, norm_gain=norm_gain, node_ids=node_ids, gates=gates, w_gate=w_gate, w_up=w_up, w_down=w_down, s_gate=s_gate, s_up=s_up, s_down=s_down)


def selection(node_rows, nodes, capacity):
    tok_count, pick_count = node_rows.shape
    node_hits = (node_rows[:, :, None] == jnp.arange(nodes, dtype=jnp.int32)).astype(jnp.int32)
    flat_hits = node_hits.reshape(tok_count * pick_count, nodes)
    earlier = jnp.cumsum(flat_hits, axis=0) - flat_hits
    slot_index = lax.optimization_barrier(jnp.sum(earlier * flat_hits, axis=1)).reshape(tok_count, pick_count)
    slot_key = node_rows * capacity + slot_index
    slots = jnp.arange(nodes * capacity, dtype=jnp.int32)
    return (slot_key[None, :, :] == slots[:, None, None]).astype(jnp.float32)

def node_work(packed):
    rows_in, gates_in, gate_w, up_w, down_w = packed
    count = rows_in.shape[0]
    width = FF_WIN // N_LOCAL
    running = jnp.zeros((count, N_LOCAL, D), jnp.float32)
    for expert in range(EXP_NODE):
        gate_proj = jnp.dot(rows_in, gate_w[expert], preferred_element_type=jnp.float32)
        up_proj = jnp.dot(rows_in, up_w[expert], preferred_element_type=jnp.float32)
        hidden = (jax.nn.silu(gate_proj) * up_proj).astype(jnp.bfloat16)
        hidden = hidden.reshape(count, N_LOCAL, width).astype(jnp.float32)
        down = down_w[expert].reshape(N_LOCAL, width, D).astype(jnp.float32)
        weight = gates_in[:, expert].astype(jnp.float32)[:, None, None]
        running = running + weight * jnp.einsum('rlf,lfd->rld', hidden, down)
    return running.astype(jnp.bfloat16).astype(jnp.float32).sum(axis=1)

def reference(attended, norm_gain, node_ids, gates, w_gate, w_up, w_down, s_gate, s_up, s_down):
    devices_part = N_NODE * N_LOCAL
    slot_total = N_NODE * CAP
    residual = attended.astype(jnp.float32)
    inv_scale = lax.rsqrt(lax.optimization_barrier(jnp.mean(residual * residual, axis=1, keepdims=True)) + 1e-06)
    normed = (residual * inv_scale * norm_gain.astype(jnp.float32)).astype(jnp.bfloat16)
    matches = jax.vmap(lambda rows_ids: selection(rows_ids, N_NODE, CAP))(node_ids.reshape(devices_part, TOK_DEV, PICK))
    selector = matches.sum(axis=3)
    normed_dev = normed.reshape(devices_part, TOK_DEV, D).astype(jnp.float32)
    buffers = jnp.einsum('bst,btd->bsd', selector, normed_dev, precision=lax.Precision.HIGHEST).astype(jnp.bfloat16)
    gates_dev = gates.reshape(devices_part, TOK_DEV, PICK, EXP_NODE).astype(jnp.float32)
    gate_buffers = jnp.einsum('bstk,btkj->bsj', matches, gates_dev, precision=lax.Precision.HIGHEST).astype(jnp.bfloat16)
    node_rows = buffers.reshape(devices_part, N_NODE, CAP, D).transpose(1, 0, 2, 3).reshape(N_NODE, devices_part * CAP, D)
    node_gates = gate_buffers.reshape(devices_part, N_NODE, CAP, EXP_NODE).transpose(1, 0, 2, 3).reshape(N_NODE, devices_part * CAP, EXP_NODE)
    node_out = lax.map(node_work, (node_rows, node_gates, w_gate.reshape(N_NODE, EXP_NODE, D, FF_WIN), w_up.reshape(N_NODE, EXP_NODE, D, FF_WIN), w_down.reshape(N_NODE, EXP_NODE, FF_WIN, D)))
    returned = node_out.reshape(N_NODE, devices_part, CAP, D).transpose(1, 0, 2, 3).reshape(devices_part, slot_total, D)
    routed = jnp.einsum('bst,bsd->btd', selector, returned, precision=lax.Precision.HIGHEST).reshape(TOKENS, D)
    shared_gate = jnp.dot(normed, s_gate, preferred_element_type=jnp.float32)
    shared_up = jnp.dot(normed, s_up, preferred_element_type=jnp.float32)
    shared_hidden = (jax.nn.silu(shared_gate) * shared_up).astype(jnp.bfloat16)
    width = SH_WIN // N_LOCAL
    shared = jnp.zeros((TOKENS, D), jnp.float32)
    for group in range(N_LOCAL):
        piece = jnp.dot(shared_hidden[:, group * width:(group + 1) * width], s_down[group * width:(group + 1) * width], preferred_element_type=jnp.float32)
        shared = shared + piece.astype(jnp.bfloat16).astype(jnp.float32)
    return (residual + routed + shared).astype(jnp.bfloat16)
```

```python
import functools

import jax
import jax.numpy as jnp
from jax import lax
from jax.experimental import pallas as pl
from jax.experimental.pallas import tpu as pltpu
from jax.sharding import PartitionSpec as P

ROWS = 128
CORES = 2
VMEM_BYTES = 14 * 2**20


def swap(x, axis, offset):
    size = lax.axis_size(axis)
    return lax.ppermute(x, axis, [(i, i ^ offset) for i in range(size)])


def resident(x):
    return pltpu.with_memory_space_constraint(x, pltpu.VMEM)


def row_loop(total, body):
    block = min(ROWS, total)
    if total == block:
        body(pl.ds(0, block))
        return

    @pl.loop(0, total // block)
    def _(index):
        body(pl.ds(pl.multiple_of(index * block, block), block))


def project(chunk_ref, gain_ref, weights, shared_weights, sums_in, sums, part):
    total, depth = chunk_ref.shape
    acc_ref, shared_ref, square_ref = sums
    start = pl.multiple_of(part * depth, depth)
    gain = gain_ref[part]
    inner = weights[0].shape[2]
    shared_inner = shared_weights[0].shape[1]

    def scaled(rows):
        values = chunk_ref[rows, :].astype(jnp.float32)
        return values, (values * gain).astype(jnp.bfloat16)

    def body(rows):
        values, lhs = scaled(rows)
        square = jnp.sum(values * values, axis=1, keepdims=True)
        square = jnp.broadcast_to(square, (square.shape[0], square_ref.shape[1]))
        if sums_in is not None:
            square = square + sums_in[2][rows, :]
        square_ref[rows, :] = square
        for expert in range(weights[0].shape[0]):
            for which, weight in enumerate(weights):
                column = (expert * 2 + which) * inner
                term = jnp.dot(
                    lhs,
                    weight[expert, pl.ds(start, depth), :],
                    preferred_element_type=jnp.float32,
                )
                if sums_in is not None:
                    term = term + sums_in[0][rows, column : column + inner]
                acc_ref[rows, column : column + inner] = term

    row_loop(total, body)
    own = shared_ref.shape[0]
    _, lhs = scaled(pl.ds(0, own))
    for which, weight in enumerate(shared_weights):
        column = which * shared_inner
        term = jnp.dot(
            lhs, weight[pl.ds(start, depth), :], preferred_element_type=jnp.float32
        )
        if sums_in is not None:
            term = term + sums_in[1][:, column : column + shared_inner]
        shared_ref[:, column : column + shared_inner] = term


def project_kernel(first, part_ref, chunk_ref, gain_ref, gate, up, s_gate, s_up, *refs):
    sums_in, sums = (None, refs) if first else (refs[:3], refs[3:])
    project(chunk_ref, gain_ref, (gate, up), (s_gate, s_up), sums_in, sums, part_ref[0])


def act(gate, up):
    return gate / (1.0 + jnp.exp(-gate)) * up


def hidden_kernel(
    width, pick, place_ref, chunk_ref, gain_ref, gate, up, s_gate, s_up,
    acc_in, shared_in, square_in, *refs
):
    *tags, hidden_ref, shared_hidden_ref, acc_ref, shared_ref, square_ref, weight_ref = refs
    part, me, node = place_ref[0], place_ref[1], place_ref[2]
    project(
        chunk_ref, gain_ref, (gate, up), (s_gate, s_up), (acc_in, shared_in, square_in),
        (acc_ref, shared_ref, square_ref), part,
    )
    experts, inner = gate.shape[0], gate.shape[2]
    total = chunk_ref.shape[0]
    own = shared_ref.shape[0]
    nodes, tokens = tags[0].shape[0], tags[0].shape[1]
    for offset, tag_ref in enumerate(tags):
        place = lax.bitwise_xor(me, offset) * tokens
        for other in range(nodes):
            tag = tag_ref[other].astype(jnp.float32)
            for expert in range(experts):
                weight = jnp.zeros((tokens, 1), jnp.float32)
                for k in range(pick):
                    column = pick + k * experts + expert
                    weight = weight + jnp.where(
                        tag[:, k : k + 1] == node.astype(jnp.float32),
                        tag[:, column : column + 1],
                        0.0,
                    )
                rows = pl.ds(pl.multiple_of(other * own + place, tokens), tokens)
                weight_ref[expert, rows, :] = jnp.broadcast_to(weight, (tokens, weight_ref.shape[2]))

    def body(rows):
        scale = lax.rsqrt(square_ref[rows, :][:, :1] / width + 1e-06)
        for expert in range(experts):
            column = expert * 2 * inner
            gate_proj = acc_ref[rows, column : column + inner] * scale
            up_proj = acc_ref[rows, column + inner : column + 2 * inner] * scale
            weight = weight_ref[expert, rows, :][:, :1]
            hidden_ref[rows, expert * inner : (expert + 1) * inner] = (
                act(gate_proj, up_proj) * weight
            ).astype(jnp.bfloat16)

    row_loop(total, body)
    shared_inner = s_gate.shape[1]
    scale = lax.rsqrt(square_ref[:own, :][:, :1] / width + 1e-06)
    gate_proj = shared_ref[:, :shared_inner] * scale
    up_proj = shared_ref[:, shared_inner:] * scale
    shared_hidden_ref[...] = act(gate_proj, up_proj).astype(jnp.bfloat16)


def down_kernel(
    columns, place_ref, hidden_ref, shared_hidden_ref, down, s_down, keep_ref, send_ref, out_ref
):
    me = place_ref[1]
    experts, inner = down.shape[0], down.shape[1]
    total, own = hidden_ref.shape[0], shared_hidden_ref.shape[0]

    def body(rows):
        term = None
        for expert in range(experts):
            more = jnp.dot(
                hidden_ref[rows, expert * inner : (expert + 1) * inner],
                down[expert, :, columns],
                preferred_element_type=jnp.float32,
            )
            term = more if term is None else term + more
        out_ref[rows, :] = term

    row_loop(total, body)
    out_ref[:own, :] += jnp.dot(
        shared_hidden_ref[...], s_down[:, columns], preferred_element_type=jnp.float32
    )
    pairs, nodes, tokens = keep_ref.shape[:3]
    for pair in range(pairs):
        for side, to_ref in enumerate((keep_ref, send_ref)):
            place = lax.bitwise_xor(me, pair * CORES + side) * tokens
            for other in range(nodes):
                rows = pl.ds(pl.multiple_of(other * own + place, tokens), tokens)
                to_ref[pair, other] = out_ref[rows, :].astype(to_ref.dtype)


def call(kernel, name, flops, read, out_shape, in_specs, scratch=(), aliases=None):
    return pl.pallas_call(
        kernel,
        out_shape=out_shape,
        in_specs=in_specs,
        out_specs=jax.tree.map(lambda _: pl.BlockSpec(memory_space=pltpu.VMEM), out_shape),
        scratch_shapes=list(scratch),
        input_output_aliases=aliases or {},
        compiler_params=pltpu.CompilerParams(vmem_limit_bytes=VMEM_BYTES),
        cost_estimate=pl.CostEstimate(flops=flops, bytes_accessed=read, transcendentals=0),
        name=name,
    )


def on_device(attended, norm_gain, node_ids, gates, w_gate, w_up, w_down, s_gate, s_up, s_down):
    node_count = lax.axis_size("node")
    local_count = lax.axis_size("local")
    pairs = local_count // CORES
    node, me = lax.axis_index("node"), lax.axis_index("local")
    own, depth = attended.shape
    tokens, pick = node_ids.shape
    experts, width, inner = w_gate.shape
    shared_inner = s_gate.shape[1]
    total = node_count * own
    smem = pl.BlockSpec(memory_space=pltpu.SMEM)
    vmem = pl.BlockSpec(memory_space=pltpu.VMEM)

    tag = jnp.concatenate(
        [node_ids.astype(jnp.bfloat16), gates.reshape(tokens, pick * experts)], axis=1
    )
    tag = jnp.pad(tag, ((0, 0), (0, 128 - tag.shape[1])))

    def gather_nodes(x):
        return jnp.concatenate([x] + [swap(x, "node", k) for k in range(1, node_count)], axis=0)

    def gather_local(x):
        columns = [x] + [swap(x, "local", k * CORES) for k in range(1, pairs)]
        return [y for column in columns for y in (column, swap(column, "local", 1))]

    chunks = gather_local(gather_nodes(attended))
    tags = gather_local(gather_nodes(tag[None]))

    gain = norm_gain.reshape(local_count, 1, depth)
    up_weights = tuple(resident(w) for w in (w_gate, w_up, s_gate, s_up))
    down_weights = tuple(resident(w) for w in (w_down, s_down))
    sums_shape = [
        jax.ShapeDtypeStruct((total, experts * 2 * inner), jnp.float32),
        jax.ShapeDtypeStruct((own, 2 * shared_inner), jnp.float32),
        jax.ShapeDtypeStruct((total, 128), jnp.float32),
    ]
    flops = 2 * depth * (total * experts * 2 * inner + own * 2 * shared_inner)
    read = 2 * depth * (experts * 2 * inner + 2 * shared_inner)
    sums = None
    for offset, chunk in enumerate(chunks[:-1]):
        part = lax.bitwise_xor(me, offset)[None]
        first = sums is None
        sums = call(
            functools.partial(project_kernel, first),
            "project",
            flops,
            read,
            sums_shape,
            [smem] + [vmem] * (6 if first else 9),
            aliases={} if first else {7: 0, 8: 1, 9: 2},
        )(part, chunk, gain, *up_weights, *(() if first else sums))
    place = jnp.stack([lax.bitwise_xor(me, local_count - 1), me, node])
    hidden, shared_hidden = call(
        functools.partial(hidden_kernel, width, pick),
        "hidden",
        flops,
        read,
        [
            jax.ShapeDtypeStruct((total, experts * inner), jnp.bfloat16),
            jax.ShapeDtypeStruct((own, shared_inner), jnp.bfloat16),
        ],
        [smem] + [vmem] * (9 + local_count),
        scratch=[pltpu.VMEM(s.shape, s.dtype) for s in sums_shape]
        + [pltpu.VMEM((experts, total, 128), jnp.float32)],
    )(place, chunks[-1], gain, *up_weights, *sums, *tags)

    slices = max(1, total // ROWS)
    step = width // slices
    results = []
    for index in range(slices):
        shape = (pairs, node_count, tokens, step)
        keep, send = call(
            functools.partial(down_kernel, slice(index * step, (index + 1) * step)),
            "down",
            2 * step * (total * experts * inner + own * shared_inner),
            2 * step * (experts * inner + shared_inner),
            [jax.ShapeDtypeStruct(shape, jnp.float32), jax.ShapeDtypeStruct(shape, jnp.bfloat16)],
            [smem] + [vmem] * 4,
            scratch=[pltpu.VMEM((total, step), jnp.float32)],
        )(place, hidden, shared_hidden, *down_weights)
        mine = keep + swap(send, "local", 1).astype(jnp.float32)
        result = mine[0]
        for k in range(1, pairs):
            result = result + swap(mine[k].astype(jnp.bfloat16), "local", k * CORES).astype(jnp.float32)
        total_here = result[0]
        for k in range(1, node_count):
            total_here = total_here + swap(result[k].astype(jnp.bfloat16), "node", k).astype(jnp.float32)
        results.append(total_here)
    mixed = jnp.concatenate(results, axis=1)

    rows = jnp.stack([lax.dynamic_slice_in_dim(c, me * tokens, tokens, 0) for c in chunks])
    bit = 1
    while bit < local_count:
        flipped = rows.reshape(local_count // (2 * bit), 2, bit, tokens, depth)[:, ::-1]
        rows = jnp.where((me & bit) != 0, flipped.reshape(rows.shape), rows)
        bit *= 2
    residual = rows.transpose(1, 0, 2).reshape(tokens, width).astype(jnp.float32)
    return (residual + mixed).astype(jnp.bfloat16)


def solution(mesh):
    in_specs = (
        P(("group", "node"), "local"),
        P(),
        P(("group", "node", "local"), None),
        P(("group", "node", "local"), None, None),
        P("node", None, "local"),
        P("node", None, "local"),
        P("node", "local", None),
        P(None, "local"),
        P(None, "local"),
        P("local", None),
    )
    out_specs = P(("group", "node", "local"), None)
    return jax.shard_map(
        on_device, mesh=mesh, in_specs=in_specs, out_specs=out_specs, check_vma=False
    )
```

```python
import functools

import jax
import jax.numpy as jnp
from jax import lax
from jax.experimental import pallas as pl
from jax.experimental.pallas import tpu as pltpu
from jax.sharding import PartitionSpec as P

ROWS = 128
LANES = 128
CORES = 2
WINDOW = 5
LATE = 2
VMEM = pl.BlockSpec(memory_space=pltpu.VMEM)
SMEM = pl.BlockSpec(memory_space=pltpu.SMEM)
ANY = pl.BlockSpec(memory_space=pl.ANY)
HBM = pl.BlockSpec(memory_space=pltpu.HBM)


def swap(x, axis, offset):
    size = lax.axis_size(axis)
    return lax.ppermute(x, axis, [(i, i ^ offset) for i in range(size)])


def in_hbm(x):
    return pltpu.with_memory_space_constraint(x, pltpu.HBM)


def row_loop(total, body):
    block = min(ROWS, total)
    if total == block:
        body(pl.ds(0, block))
        return

    @pl.loop(0, total // block)
    def _(index):
        body(pl.ds(pl.multiple_of(index * block, block), block))


def pack_kernel(pick, experts, place_ref, *refs):
    sources, (block_ref, rows_ref, ids_ref, gates_ref, sems) = refs[:3], refs[3:]
    own, depth = rows_ref.shape
    moves = [
        pltpu.make_async_copy(source, target, sems.at[index])
        for index, (source, target) in enumerate(zip(sources, (rows_ref, ids_ref, gates_ref)))
    ]
    for move in moves:
        move.start()
    for move in moves:
        move.wait()
    tokens = ids_ref.shape[1]
    diagonal = lax.broadcasted_iota(jnp.int32, (tokens, tokens), 0) == lax.broadcasted_iota(
        jnp.int32, (tokens, tokens), 1
    )
    lane = lax.broadcasted_iota(jnp.int32, (tokens, LANES), 1)
    tag = jnp.zeros((tokens, LANES), jnp.float32)
    for index in range(pick * (1 + experts)):
        ref, row = (ids_ref, index) if index < pick else (gates_ref, index - pick)
        values = ref[row : row + 1, :].astype(jnp.float32)
        column = jnp.sum(jnp.where(diagonal, values, 0.0), axis=1, keepdims=True)
        tag = jnp.where(lane == index, column, tag)
    tags = jnp.concatenate([tag] * (own // tokens), axis=0)
    row = lax.broadcasted_iota(jnp.int32, (own, LANES), 0)
    first = place_ref[0] * tokens
    mine = (row >= first) & (row < first + tokens)
    block_ref[:, :depth] = rows_ref[...]
    block_ref[:, depth:] = jnp.where(mine, tags, 0.0).astype(jnp.bfloat16)


class Queue:
    def __init__(self, moves):
        self.moves, self.waited = moves, 0
        for move in moves[:WINDOW]:
            move.start()

    def wait(self):
        self.moves[self.waited].wait()
        if self.waited + WINDOW < len(self.moves):
            self.moves[self.waited + WINDOW].start()
        self.waited += 1


def weight_moves(parts, weights, buffers, sems):
    gate, up, s_gate, s_up = weights
    buffer, shared_buffer = buffers
    experts, depth = gate.shape[0], buffer.shape[2]
    moves = []

    def move(source, target):
        moves.append(pltpu.make_async_copy(source, target, sems.at[len(moves)]))

    blocks = [pl.ds(pl.multiple_of(part * depth, depth), depth) for part in parts]
    for slot in range(experts * 2):
        for index, rows in enumerate(blocks):
            move((gate, up)[slot % 2].at[slot // 2, rows, :], buffer.at[index, slot])
    for which, weight in enumerate((s_gate, s_up)):
        for index, rows in enumerate(blocks):
            move(weight.at[rows, :], shared_buffer.at[index, which])
    return moves


def scaled_rows(chunk_ref, gain, rows):
    values = chunk_ref[rows, : gain.shape[1]].astype(jnp.float32)
    return values, (values * gain).astype(jnp.bfloat16)


def square_sums(chunk_ref, gain, lhs_ref, square_ref, square_in):
    def body(rows):
        values, lhs = scaled_rows(chunk_ref, gain, rows)
        lhs_ref[rows, :] = lhs
        square = jnp.sum(values * values, axis=1, keepdims=True)
        square = jnp.broadcast_to(square, (square.shape[0], LANES))
        square_ref[rows, :] = square if square_in is None else square + square_in[rows, :]

    row_loop(chunk_ref.shape[0], body)


def project_kernel(first, extra, part_ref, chunk_ref, gain_ref, *refs):
    weights, refs = refs[:4], refs[4 + extra :]
    (acc_in, shared_in, square_in), refs = ((None,) * 3, refs) if first else (refs[:3], refs[3:])
    acc_ref, shared_ref, square_ref, lhs_ref, buffer, shared_buffer, sems = refs
    part = part_ref[0]
    queue = Queue(weight_moves([part], weights, (buffer, shared_buffer), sems))
    square_sums(chunk_ref, gain_ref[part], lhs_ref, square_ref, square_in)
    inner, shared_inner = buffer.shape[3], shared_buffer.shape[3]
    for slot in range(buffer.shape[1]):
        queue.wait()
        columns = slice(slot * inner, (slot + 1) * inner)

        def body(rows):
            term = jnp.dot(lhs_ref[rows, :], buffer[0, slot], preferred_element_type=jnp.float32)
            acc_ref[rows, columns] = term if first else term + acc_in[rows, columns]

        row_loop(chunk_ref.shape[0], body)
    own = shared_ref.shape[0]
    for which in range(2):
        queue.wait()
        columns = slice(which * shared_inner, (which + 1) * shared_inner)
        term = jnp.dot(
            lhs_ref[:own, :], shared_buffer[0, which], preferred_element_type=jnp.float32
        )
        shared_ref[:, columns] = term if first else term + shared_in[:, columns]


def join_kernel(count, *refs):
    out_ref = refs[-1]
    start = 0
    for ref in refs[:count]:
        out_ref[start : start + ref.shape[0], :] = ref[...]
        start += ref.shape[0]


def relay_kernel(half, mine_ref, *refs):
    pairs, nodes = mine_ref.shape[:2]
    came, sums, near = refs[: pairs - 1], refs[pairs - 1 : pairs - 1 + nodes - half], refs[pairs - 1 + nodes - half :]
    for index, sum_ref in enumerate(sums):
        total = mine_ref[0, half + index]
        for ref in came:
            total = total + ref[index].astype(jnp.float32)
        sum_ref[...] = total.astype(jnp.bfloat16)
    for pair, ref in enumerate(near):
        ref[...] = mine_ref[pair + 1, :half].astype(jnp.bfloat16)


def act(gate, up):
    return gate / (1.0 + jnp.exp(-gate)) * up


def row_share(tag, node, pick, experts, expert):
    share = jnp.zeros((tag.shape[0], 1), jnp.float32)
    for k in range(pick):
        column = pick + k * experts + expert
        share = share + jnp.where(
            tag[:, k : k + 1] == node.astype(jnp.float32), tag[:, column : column + 1], 0.0
        )
    return share


def down_part(me, hidden_ref, shared_hidden_ref, wait, down, s_down, out_ref, keep_ref, send_ref):
    experts, inner = down.shape[0], down.shape[1]
    own = shared_hidden_ref.shape[0]
    for expert in range(experts):
        wait()

        def body(rows):
            term = jnp.dot(
                hidden_ref[rows, expert * inner : (expert + 1) * inner],
                down[expert],
                preferred_element_type=jnp.float32,
            )
            out_ref[rows, :] = term if expert == 0 else term + out_ref[rows, :]

        row_loop(hidden_ref.shape[0], body)
    wait()
    out_ref[:own, :] += jnp.dot(
        shared_hidden_ref[...], s_down[...], preferred_element_type=jnp.float32
    )
    pairs, nodes, tokens = keep_ref.shape[:3]
    for pair in range(pairs):
        for side, to_ref in enumerate((keep_ref, send_ref)):
            place = lax.bitwise_xor(me, pair * CORES + side) * tokens
            for other in range(nodes):
                rows = pl.ds(pl.multiple_of(other * own + place, tokens), tokens)
                to_ref[pair, other] = out_ref[rows, :].astype(to_ref.dtype)


def down_moves(columns, down, s_down, buffer, shared_buffer, sems, base):
    experts = down.shape[0]
    moves = [
        pltpu.make_async_copy(down.at[e, :, columns], buffer.at[e], sems.at[base + e])
        for e in range(experts)
    ]
    return moves + [
        pltpu.make_async_copy(s_down.at[:, columns], shared_buffer, sems.at[base + experts])
    ]


def finish_kernel(
    width, pick, columns, part_count, place_ref, gain_ref, gate, up, s_gate, s_up,
    acc_in, shared_in, square_in, down, s_down, *refs
):
    chunks, refs = refs[:part_count], refs[part_count:]
    (
        hidden_ref, shared_hidden_ref, keep_ref, send_ref,
        lhs_ref, square_ref, buffer, shared_buffer, down_buffer, s_down_buffer, out_ref, sems,
    ) = refs
    me, node = place_ref[0], place_ref[1]
    late = buffer.shape[0]
    parts = [lax.bitwise_xor(me, part_count - late + index) for index in range(late)]
    moves = weight_moves(parts, (gate, up, s_gate, s_up), (buffer, shared_buffer), sems)
    moves += down_moves(columns, down, s_down, down_buffer, s_down_buffer, sems, len(moves))
    queue = Queue(moves)
    experts, inner, shared_inner = gate.shape[0], gate.shape[2], s_gate.shape[1]
    own, depth = shared_in.shape[0], gain_ref.shape[2]
    for index, part in enumerate(parts):
        square_sums(
            chunks[index - late], gain_ref[part], lhs_ref.at[index], square_ref,
            square_ref if index else square_in,
        )
    for expert in range(experts):

        def body(rows):
            tag = sum(chunk[rows, depth:].astype(jnp.float32) for chunk in chunks)
            scale = lax.rsqrt(square_ref[rows, :][:, :1] / width + 1e-06)
            projs = []
            for slot in (2 * expert, 2 * expert + 1):
                term = acc_in[rows, slot * inner : (slot + 1) * inner]
                for index in range(late):
                    term = term + jnp.dot(
                        lhs_ref[index, rows, :],
                        buffer[index, slot],
                        preferred_element_type=jnp.float32,
                    )
                projs.append(term * scale)
            share = row_share(tag, node, pick, experts, expert)
            hidden_ref[rows, expert * inner : (expert + 1) * inner] = (
                act(*projs) * share
            ).astype(jnp.bfloat16)

        for _ in range(2 * late):
            queue.wait()
        row_loop(chunks[-1].shape[0], body)
    scale = lax.rsqrt(square_ref[:own, :][:, :1] / width + 1e-06)
    projs = []
    for which in range(2):
        term = shared_in[:, which * shared_inner : (which + 1) * shared_inner]
        for index in range(late):
            queue.wait()
            term = term + jnp.dot(
                lhs_ref[index, :own, :],
                shared_buffer[index, which],
                preferred_element_type=jnp.float32,
            )
        projs.append(term * scale)
    shared_hidden_ref[...] = act(*projs).astype(jnp.bfloat16)
    down_part(
        me, hidden_ref, shared_hidden_ref, queue.wait, down_buffer, s_down_buffer,
        out_ref, keep_ref, send_ref,
    )


def down_kernel(columns, place_ref, hidden_ref, shared_hidden_ref, down, s_down, keep_ref, send_ref, buffer, shared_buffer, out_ref, sems):
    queue = Queue(down_moves(columns, down, s_down, buffer, shared_buffer, sems, 0))
    down_part(
        place_ref[0], hidden_ref, shared_hidden_ref, queue.wait, buffer, shared_buffer,
        out_ref, keep_ref, send_ref,
    )


def call(kernel, name, out_shape, in_specs, scratch, args, flops=0, read=0, aliases=None):
    held = [a for a, spec in zip(args, in_specs) if spec is VMEM] + list(out_shape)
    held += [s for s in scratch if hasattr(s, "dtype") and s.memory_space == pltpu.VMEM]
    size = 0
    for array in held:
        count = jnp.dtype(array.dtype).itemsize
        for extent in array.shape:
            count *= extent
        size += count
    return pl.pallas_call(
        kernel,
        out_shape=out_shape,
        in_specs=in_specs,
        out_specs=[VMEM] * len(out_shape),
        scratch_shapes=scratch,
        input_output_aliases=aliases or {},
        compiler_params=pltpu.CompilerParams(vmem_limit_bytes=size + 8 * 2**20),
        cost_estimate=pl.CostEstimate(flops=flops, bytes_accessed=read, transcendentals=0),
        name=name,
    )(*args)


def on_device(attended, norm_gain, node_ids, gates, w_gate, w_up, w_down, s_gate, s_up, s_down):
    node_count = lax.axis_size("node")
    local_count = lax.axis_size("local")
    pairs = local_count // CORES
    node, me = lax.axis_index("node"), lax.axis_index("local")
    own, depth = attended.shape
    tokens, pick = node_ids.shape
    experts, width, inner = w_gate.shape
    shared_inner = s_gate.shape[1]
    total = node_count * own
    up_weights = tuple(in_hbm(w) for w in (w_gate, w_up, s_gate, s_up))
    down_weights = tuple(in_hbm(w) for w in (w_down, s_down))
    f32, bf16 = jnp.float32, jnp.bfloat16

    inputs = (
        in_hbm(attended),
        in_hbm(node_ids.T),
        in_hbm(gates.transpose(1, 2, 0).reshape(pick * experts, tokens)),
    )
    (block,) = call(
        functools.partial(pack_kernel, pick, experts),
        "pack",
        [jax.ShapeDtypeStruct((own, depth + LANES), bf16)],
        [SMEM, HBM, HBM, HBM],
        [pltpu.VMEM(x.shape, x.dtype) for x in inputs] + [pltpu.SemaphoreType.DMA((3,))],
        (me[None], *inputs),
    )
    blocks = [block] + [swap(block, "node", k) for k in range(1, node_count)]
    rest = jnp.concatenate(blocks[1:], axis=0)
    column = jnp.concatenate([block, rest], axis=0)
    chunks = [column, swap(column, "local", 1)]

    def neighbour(k, sums):
        (column,) = call(
            functools.partial(join_kernel, 2),
            "join",
            [jax.ShapeDtypeStruct(chunks[0].shape, bf16)],
            [VMEM, VMEM, ANY],
            [],
            (first_rows[k - 1], other_rows[k - 1], sums[2]),
        )
        return [column, swap(column, "local", 1)]

    first_rows = [swap(block, "local", k * CORES) for k in range(1, pairs)]
    other_rows = [swap(rest, "local", k * CORES) for k in range(1, pairs)]

    gain = norm_gain.reshape(local_count, 1, depth)
    sums_shape = [
        jax.ShapeDtypeStruct((total, experts * 2 * inner), f32),
        jax.ShapeDtypeStruct((own, 2 * shared_inner), f32),
        jax.ShapeDtypeStruct((total, LANES), f32),
    ]
    flops = 2 * depth * (total * experts * 2 * inner + own * 2 * shared_inner)
    read = 2 * depth * (experts * 2 * inner + 2 * shared_inner)
    weight_scratch = [
        pltpu.VMEM((1, experts * 2, depth, inner), bf16),
        pltpu.VMEM((1, 2, depth, shared_inner), bf16),
    ]
    lhs_scratch = pltpu.VMEM((total, depth), bf16)
    moves = experts * 2 + 2
    sums = None
    for offset in range(local_count - LATE):
        first = sums is None
        if offset == CORES - 1:
            for k in range(1, pairs):
                chunks += neighbour(k, sums)
        args = (lax.bitwise_xor(me, offset)[None], chunks[offset], gain, *up_weights)
        more = tuple(first_rows) if first else tuple(sums)
        sums = call(
            functools.partial(project_kernel, first, len(more) if first else 0),
            "project",
            sums_shape,
            [SMEM, VMEM, VMEM] + [HBM] * 4 + [ANY if first else VMEM] * len(more),
            [lhs_scratch, *weight_scratch, pltpu.SemaphoreType.DMA((moves,))],
            args + more,
            flops,
            read,
            aliases={} if first else {7: 0, 8: 1, 9: 2},
        )
    place = jnp.stack([me, node])

    slices = max(1, total // ROWS)
    step = width // slices
    shape = (pairs, node_count, tokens, step)
    out_shape = [jax.ShapeDtypeStruct(shape, f32), jax.ShapeDtypeStruct(shape, bf16)]
    down_scratch = [
        pltpu.VMEM((experts, inner, step), bf16),
        pltpu.VMEM((shared_inner, step), bf16),
        pltpu.VMEM((total, step), f32),
    ]
    down_flops = 2 * step * (total * experts * inner + own * shared_inner)
    down_read = 2 * step * (experts * inner + shared_inner)
    partials = []
    for index in range(slices):
        columns = slice(index * step, (index + 1) * step)
        if index == 0:
            hidden, shared_hidden, keep, send = call(
                functools.partial(finish_kernel, width, pick, columns, local_count),
                "finish",
                [
                    jax.ShapeDtypeStruct((total, experts * inner), bf16),
                    jax.ShapeDtypeStruct((own, shared_inner), bf16),
                ]
                + out_shape,
                [SMEM, VMEM] + [HBM] * 4 + [VMEM] * 3 + [HBM] * 2 + [VMEM] * local_count,
                [
                    pltpu.VMEM((LATE, total, depth), bf16),
                    pltpu.VMEM((total, LANES), f32),
                    *(pltpu.VMEM((LATE, *w.shape[1:]), bf16) for w in weight_scratch),
                    *down_scratch,
                    pltpu.SemaphoreType.DMA((LATE * moves + experts + 1,)),
                ],
                (place, gain, *up_weights, *sums, *down_weights, *chunks),
                flops + down_flops,
                read + down_read,
            )
        else:
            keep, send = call(
                functools.partial(down_kernel, columns),
                "down",
                out_shape,
                [SMEM, VMEM, VMEM, HBM, HBM],
                [*down_scratch, pltpu.SemaphoreType.DMA((experts + 1,))],
                (place, hidden, shared_hidden, *down_weights),
                down_flops,
                down_read,
            )
        partials.append((keep, send))

    half = node_count // 2
    results = []
    for keep, send in partials:
        mine = keep + swap(send, "local", 1).astype(f32)
        came = [swap(mine[k, half:].astype(bf16), "local", k * CORES) for k in range(1, pairs)]
        rows_shape = jax.ShapeDtypeStruct((tokens, step), bf16)
        near_shape = jax.ShapeDtypeStruct((half, tokens, step), bf16)
        out = call(
            functools.partial(relay_kernel, half),
            "relay",
            [rows_shape] * (node_count - half) + [near_shape] * (pairs - 1),
            [VMEM] * pairs,
            [],
            (mine, *came),
        )
        far, near = out[: node_count - half], out[node_count - half :]
        near_came = [swap(x, "local", k * CORES).astype(f32) for k, x in enumerate(near, 1)]
        far_came = [swap(x, "node", half + k).astype(f32) for k, x in enumerate(far)]
        result = sum(near_came, mine[0, :half])
        total_here = result[0]
        for k in range(1, half):
            total_here = total_here + swap(result[k].astype(bf16), "node", k).astype(f32)
        total_here = sum(far_came, total_here)
        results.append(total_here)
    mixed = jnp.concatenate(results, axis=1)

    rows = jnp.stack(
        [lax.dynamic_slice(c, (me * tokens, 0), (tokens, depth)) for c in chunks]
    )
    bit = 1
    while bit < local_count:
        flipped = rows.reshape(local_count // (2 * bit), 2, bit, tokens, depth)[:, ::-1]
        rows = jnp.where((me & bit) != 0, flipped.reshape(rows.shape), rows)
        bit *= 2
    residual = rows.transpose(1, 0, 2).reshape(tokens, width).astype(jnp.float32)
    return (residual + mixed).astype(jnp.bfloat16)


def solution(mesh):
    in_specs = (
        P(("group", "node"), "local"),
        P(),
        P(("group", "node", "local"), None),
        P(("group", "node", "local"), None, None),
        P("node", None, "local"),
        P("node", None, "local"),
        P("node", "local", None),
        P(None, "local"),
        P(None, "local"),
        P("local", None),
    )
    out_specs = P(("group", "node", "local"), None)
    return jax.shard_map(
        on_device, mesh=mesh, in_specs=in_specs, out_specs=out_specs, check_vma=False
    )
```

```python
import functools

import jax
import jax.numpy as jnp
from jax import lax
from jax.experimental import pallas as pl
from jax.experimental.pallas import tpu as pltpu
from jax.sharding import PartitionSpec as P

ROWS = 128
LANES = 128
CORES = 2
WINDOW = 40
LATE = 2
VMEM = pl.BlockSpec(memory_space=pltpu.VMEM)
SMEM = pl.BlockSpec(memory_space=pltpu.SMEM)
ANY = pl.BlockSpec(memory_space=pl.ANY)
HBM = pl.BlockSpec(memory_space=pltpu.HBM)


def swap(x, axis, offset):
    size = lax.axis_size(axis)
    return lax.ppermute(x, axis, [(i, i ^ offset) for i in range(size)])


def in_hbm(x):
    return pltpu.with_memory_space_constraint(x, pltpu.HBM)


def row_loop(total, body):
    block = min(ROWS, total)
    if total == block:
        body(pl.ds(0, block))
        return

    @pl.loop(0, total // block)
    def _(index):
        body(pl.ds(pl.multiple_of(index * block, block), block))


def pack_kernel(pick, experts, place_ref, *refs):
    sources, (block_ref, gain_ref, rows_ref, ids_ref, gates_ref, sems) = refs[:4], refs[4:]
    own, depth = rows_ref.shape
    moves = [
        pltpu.make_async_copy(source, target, sems.at[index])
        for index, (source, target) in enumerate(zip(sources, (rows_ref, ids_ref, gates_ref, gain_ref)))
    ]
    for move in moves:
        move.start()
    for move in moves:
        move.wait()
    tokens = ids_ref.shape[1]
    diagonal = lax.broadcasted_iota(jnp.int32, (tokens, tokens), 0) == lax.broadcasted_iota(
        jnp.int32, (tokens, tokens), 1
    )
    lane = lax.broadcasted_iota(jnp.int32, (tokens, LANES), 1)
    tag = jnp.zeros((tokens, LANES), jnp.float32)
    for index in range(pick * (1 + experts)):
        ref, row = (ids_ref, index) if index < pick else (gates_ref, index - pick)
        values = ref[row : row + 1, :].astype(jnp.float32)
        column = jnp.sum(jnp.where(diagonal, values, 0.0), axis=1, keepdims=True)
        tag = jnp.where(lane == index, column, tag)
    tags = jnp.concatenate([tag] * (own // tokens), axis=0)
    row = lax.broadcasted_iota(jnp.int32, (own, LANES), 0)
    first = place_ref[0] * tokens
    mine = (row >= first) & (row < first + tokens)
    block_ref[:, :depth] = rows_ref[...]
    block_ref[:, depth:] = jnp.where(mine, tags, 0.0).astype(jnp.bfloat16)


class Queue:
    def __init__(self, moves):
        self.moves, self.waited = moves, 0
        for move in moves[:WINDOW]:
            move.start()

    def wait(self):
        self.moves[self.waited].wait()
        if self.waited + WINDOW < len(self.moves):
            self.moves[self.waited + WINDOW].start()
        self.waited += 1


def weight_moves(parts, weights, buffers, sems):
    gate, up, s_gate, s_up = weights
    buffer, shared_buffer = buffers
    experts, depth = gate.shape[0], buffer.shape[2]
    moves = []

    def move(source, target):
        moves.append(pltpu.make_async_copy(source, target, sems.at[len(moves)]))

    blocks = [pl.ds(pl.multiple_of(part * depth, depth), depth) for part in parts]
    for which, weight in enumerate((s_gate, s_up)):
        for index, rows in enumerate(blocks):
            move(weight.at[rows, :], shared_buffer.at[index, which])
    for slot in range(experts * 2):
        for index, rows in enumerate(blocks):
            move((gate, up)[slot % 2].at[slot // 2, rows, :], buffer.at[index, slot])
    return moves


def scaled_rows(chunk_ref, gain, rows):
    values = chunk_ref[rows, : gain.shape[1]].astype(jnp.float32)
    return values, (values * gain).astype(jnp.bfloat16)


def square_sums(chunk_ref, gain, lhs_ref, square_ref, square_in):
    def body(rows):
        values, lhs = scaled_rows(chunk_ref, gain, rows)
        lhs_ref[rows, :] = lhs
        square = jnp.sum(values * values, axis=1, keepdims=True)
        square = jnp.broadcast_to(square, (square.shape[0], LANES))
        square_ref[rows, :] = square if square_in is None else square + square_in[rows, :]

    row_loop(chunk_ref.shape[0], body)


def project_kernel(first, extra, part_ref, chunk_ref, gain_ref, *refs):
    weights, refs = refs[:4], refs[4 + extra :]
    (acc_in, shared_in, square_in), refs = ((None,) * 3, refs) if first else (refs[:3], refs[3:])
    acc_ref, shared_ref, square_ref, lhs_ref, buffer, shared_buffer, sems = refs
    part = part_ref[0]
    queue = Queue(weight_moves([part], weights, (buffer, shared_buffer), sems))
    square_sums(chunk_ref, gain_ref[part], lhs_ref, square_ref, square_in)
    inner, shared_inner = buffer.shape[3], shared_buffer.shape[3]
    own = shared_ref.shape[0]
    for which in range(2):
        queue.wait()
        columns = slice(which * shared_inner, (which + 1) * shared_inner)
        term = jnp.dot(
            lhs_ref[:own, :], shared_buffer[0, which], preferred_element_type=jnp.float32
        )
        shared_ref[:, columns] = term if first else term + shared_in[:, columns]
    for slot in range(buffer.shape[1]):
        queue.wait()
        columns = slice(slot * inner, (slot + 1) * inner)

        def body(rows):
            term = jnp.dot(lhs_ref[rows, :], buffer[0, slot], preferred_element_type=jnp.float32)
            acc_ref[rows, columns] = term if first else term + acc_in[rows, columns]

        row_loop(chunk_ref.shape[0], body)


def join_kernel(count, *refs):
    out_ref = refs[-1]
    start = 0
    for ref in refs[:count]:
        out_ref[start : start + ref.shape[0], :] = ref[...]
        start += ref.shape[0]


def relay_kernel(far_ref, near_ref, *refs):
    pairs, nodes = far_ref.shape[:2]
    came, sums, near = refs[: pairs - 1], refs[pairs - 1 : pairs - 1 + nodes], refs[pairs - 1 + nodes :]
    for index, sum_ref in enumerate(sums):
        total = far_ref[0, index]
        for ref in came:
            total = total + ref[index].astype(jnp.float32)
        sum_ref[...] = total.astype(jnp.bfloat16)
    for pair, ref in enumerate(near):
        ref[...] = near_ref[pair + 1].astype(jnp.bfloat16)


def act(gate, up):
    return gate / (1.0 + jnp.exp(-gate)) * up


def row_share(tag, node, pick, experts, expert):
    share = jnp.zeros((tag.shape[0], 1), jnp.float32)
    for k in range(pick):
        column = pick + k * experts + expert
        share = share + jnp.where(
            tag[:, k : k + 1] == node.astype(jnp.float32), tag[:, column : column + 1], 0.0
        )
    return share


def row_blocks(total):
    block = min(ROWS, total)
    return [slice(start, start + block) for start in range(0, total, block)]


def down_expert(hidden_ref, shared_hidden_ref, expert, first, down, s_down, out_ref):
    inner = down.shape[1]
    count, _, step = out_ref.shape
    own = shared_hidden_ref.shape[0]
    for index in range(count):
        taken = slice(first + index * step, first + (index + 1) * step)
        for rows in row_blocks(hidden_ref.shape[0]):
            term = jnp.dot(
                hidden_ref[rows, expert * inner : (expert + 1) * inner],
                down[expert, :, taken],
                preferred_element_type=jnp.float32,
            )
            out_ref[index, rows, :] = term if expert == 0 else term + out_ref[index, rows, :]
        if expert == 0:
            out_ref[index, :own, :] += jnp.dot(
                shared_hidden_ref[...], s_down[:, taken], preferred_element_type=jnp.float32
            )


def leave(me, own, out_ref, outs):
    count, _, step = out_ref.shape
    keep_far, keep_near, send_far, send_near = outs
    pairs, near, tokens = keep_near.shape[:3]
    for index in range(count):
        columns = slice(index * step, (index + 1) * step)
        for pair in range(pairs):
            for side, to_refs in enumerate(((keep_near, keep_far), (send_near, send_far))):
                place = lax.bitwise_xor(me, pair * CORES + side) * tokens
                for other in range(near + keep_far.shape[1]):
                    rows = pl.ds(pl.multiple_of(other * own + place, tokens), tokens)
                    to_ref = to_refs[other >= near]
                    to_ref[pair, other % near, :, columns] = out_ref[index, rows, :].astype(to_ref.dtype)


def finish_kernel(
    width, pick, part_count, place_ref, gain_ref, gate, up, s_gate, s_up,
    acc_in, shared_in, square_in, down, s_down, *refs
):
    chunks, refs = refs[:part_count], refs[part_count:]
    (
        hidden_ref, shared_hidden_ref, *outs,
        lhs_ref, square_ref, share_ref, buffer, shared_buffer, out_ref, sems,
    ) = refs
    me, node = place_ref[0], place_ref[1]
    late = buffer.shape[0]
    parts = [lax.bitwise_xor(me, part_count - late + index) for index in range(late)]
    moves = weight_moves(parts, (gate, up, s_gate, s_up), (buffer, shared_buffer), sems)
    queue = Queue(moves)
    experts, inner, shared_inner = gate.shape[0], gate.shape[2], s_gate.shape[1]
    own, depth = shared_in.shape[0], gain_ref.shape[2]
    for index, part in enumerate(parts):
        square_sums(
            chunks[index - late], gain_ref[part], lhs_ref.at[index], square_ref,
            square_ref if index else square_in,
        )
    blocks = row_blocks(chunks[-1].shape[0])
    for rows in blocks:
        tag = sum(chunk[rows, depth:].astype(jnp.float32) for chunk in chunks)
        for expert in range(experts):
            share = row_share(tag, node, pick, experts, expert)
            share_ref[expert, rows, :] = jnp.broadcast_to(share, (share.shape[0], LANES))
        square_ref[rows, :] = lax.rsqrt(square_ref[rows, :] / width + 1e-06)

    def project(rows_list, before, weights):
        terms = [before[rows] for rows in rows_list]
        for index in range(late):
            queue.wait()
            for at, rows in enumerate(rows_list):
                terms[at] = terms[at] + jnp.dot(
                    lhs_ref[index, rows, :], weights(index), preferred_element_type=jnp.float32
                )
        return [term * square_ref[rows, :][:, :1] for term, rows in zip(terms, rows_list)]

    class Columns:
        def __init__(self, ref, start, count):
            self.ref, self.columns = ref, slice(start, start + count)

        def __getitem__(self, rows):
            return self.ref[rows, self.columns]

    projs = []
    for which in range(2):
        before = Columns(shared_in, which * shared_inner, shared_inner)
        projs += project([slice(0, own)], before, lambda index: shared_buffer[index, which])
    shared_hidden_ref[...] = act(*projs).astype(jnp.bfloat16)
    for expert in range(experts):
        projs = []
        for slot in (2 * expert, 2 * expert + 1):
            before = Columns(acc_in, slot * inner, inner)
            projs.append(project(blocks, before, lambda index: buffer[index, slot]))
        for rows, gate_proj, up_proj in zip(blocks, *projs):
            hidden_ref[rows, expert * inner : (expert + 1) * inner] = (
                act(gate_proj, up_proj) * share_ref[expert, rows, :][:, :1]
            ).astype(jnp.bfloat16)
        down_expert(hidden_ref, shared_hidden_ref, expert, 0, down, s_down, out_ref)
    leave(me, own, out_ref, outs)


def down_kernel(first, place_ref, hidden_ref, shared_hidden_ref, down, s_down, *refs):
    for expert in range(down.shape[0]):
        down_expert(hidden_ref, shared_hidden_ref, expert, first, down, s_down, refs[-1])
    leave(place_ref[0], shared_hidden_ref.shape[0], refs[-1], refs[:4])


def call(kernel, name, out_shape, in_specs, scratch, args, flops=0, read=0, aliases=None):
    held = [a for a, spec in zip(args, in_specs) if spec is VMEM and a.ndim < 3] + list(out_shape)
    held += [s for s in scratch if hasattr(s, "dtype") and s.memory_space == pltpu.VMEM]
    size = 0
    for array in held:
        count = jnp.dtype(array.dtype).itemsize
        for extent in array.shape:
            count *= extent
        size += count
    return pl.pallas_call(
        kernel,
        out_shape=out_shape,
        in_specs=in_specs,
        out_specs=[VMEM] * len(out_shape),
        scratch_shapes=scratch,
        input_output_aliases=aliases or {},
        compiler_params=pltpu.CompilerParams(vmem_limit_bytes=size + 8 * 2**20),
        cost_estimate=pl.CostEstimate(flops=flops, bytes_accessed=read, transcendentals=0),
        name=name,
    )(*args)


def on_device(attended, norm_gain, node_ids, gates, w_gate, w_up, w_down, s_gate, s_up, s_down):
    node_count = lax.axis_size("node")
    local_count = lax.axis_size("local")
    pairs = local_count // CORES
    node, me = lax.axis_index("node"), lax.axis_index("local")
    own, depth = attended.shape
    tokens, pick = node_ids.shape
    experts, width, inner = w_gate.shape
    shared_inner = s_gate.shape[1]
    total = node_count * own
    up_weights = tuple(in_hbm(w) for w in (w_gate, w_up, s_gate, s_up))
    down_weights = (w_down, s_down)
    f32, bf16 = jnp.float32, jnp.bfloat16

    inputs = (
        in_hbm(attended),
        in_hbm(node_ids.T),
        in_hbm(gates.transpose(1, 2, 0).reshape(pick * experts, tokens)),
        in_hbm(norm_gain.reshape(local_count, 1, depth)),
    )
    block, gain = call(
        functools.partial(pack_kernel, pick, experts),
        "pack",
        [
            jax.ShapeDtypeStruct((own, depth + LANES), bf16),
            jax.ShapeDtypeStruct((local_count, 1, depth), f32),
        ],
        [SMEM] + [HBM] * 4,
        [pltpu.VMEM(x.shape, x.dtype) for x in inputs[:3]] + [pltpu.SemaphoreType.DMA((4,))],
        (me[None], *inputs),
        flops=4 * 10**10,
    )
    blocks = [block] + [swap(block, "node", k) for k in range(1, node_count)]
    rest = jnp.concatenate(blocks[1:], axis=0)
    column = jnp.concatenate([block, rest], axis=0)
    chunks = [column, swap(column, "local", 1)]

    def neighbour(k, sums):
        (column,) = call(
            functools.partial(join_kernel, 2),
            "join",
            [jax.ShapeDtypeStruct(chunks[0].shape, bf16)],
            [VMEM, VMEM, ANY],
            [],
            (first_rows[k - 1], other_rows[k - 1], sums[2]),
        )
        return [column, swap(column, "local", 1)]

    first_rows = [swap(block, "local", k * CORES) for k in range(1, pairs)]
    other_rows = [swap(rest, "local", k * CORES) for k in range(1, pairs)]

    sums_shape = [
        jax.ShapeDtypeStruct((total, experts * 2 * inner), f32),
        jax.ShapeDtypeStruct((own, 2 * shared_inner), f32),
        jax.ShapeDtypeStruct((total, LANES), f32),
    ]
    flops = 2 * depth * (total * experts * 2 * inner + own * 2 * shared_inner)
    read = 2 * depth * (experts * 2 * inner + 2 * shared_inner)
    weight_scratch = [
        pltpu.VMEM((1, experts * 2, depth, inner), bf16),
        pltpu.VMEM((1, 2, depth, shared_inner), bf16),
    ]
    lhs_scratch = pltpu.VMEM((total, depth), bf16)
    moves = experts * 2 + 2
    sums = None
    for offset in range(local_count - LATE):
        first = sums is None
        if offset == CORES - 1:
            for k in range(1, pairs):
                chunks += neighbour(k, sums)
        args = (lax.bitwise_xor(me, offset)[None], chunks[offset], gain, *up_weights)
        more = tuple(first_rows) if first else tuple(sums)
        sums = call(
            functools.partial(project_kernel, first, len(more) if first else 0),
            "project",
            sums_shape,
            [SMEM, VMEM, VMEM] + [HBM] * 4 + [ANY if first else VMEM] * len(more),
            [lhs_scratch, *weight_scratch, pltpu.SemaphoreType.DMA((moves,))],
            args + more,
            flops,
            read,
            aliases={} if first else {7: 0, 8: 1, 9: 2},
        )
    place = jnp.stack([me, node])

    slices = max(1, total // ROWS)
    step = width // slices
    half = node_count // 2
    out_shape = [
        jax.ShapeDtypeStruct((pairs, half, tokens, step), dtype)
        for dtype in (f32, f32, bf16, bf16)
    ]
    pieces = max(1, step // (10 * LANES))
    down_scratch = [
        pltpu.VMEM((pieces, total, step // pieces), f32),
    ]
    down_flops = 2 * step * (total * experts * inner + own * shared_inner)
    down_read = 2 * step * (experts * inner + shared_inner)
    partials = []
    for index in range(slices):
        if index == 0:
            hidden, shared_hidden, *out = call(
                functools.partial(finish_kernel, width, pick, local_count),
                "finish",
                [
                    jax.ShapeDtypeStruct((total, experts * inner), bf16),
                    jax.ShapeDtypeStruct((own, shared_inner), bf16),
                ]
                + out_shape,
                [SMEM, VMEM] + [HBM] * 4 + [VMEM] * (5 + local_count),
                [
                    pltpu.VMEM((LATE, total, depth), bf16),
                    pltpu.VMEM((total, LANES), f32),
                    pltpu.VMEM((experts, total, LANES), f32),
                    *(pltpu.VMEM((LATE, *w.shape[1:]), bf16) for w in weight_scratch),
                    *down_scratch,
                    pltpu.SemaphoreType.DMA((LATE * moves,)),
                ],
                (place, gain, *up_weights, *sums, *down_weights, *chunks),
                flops + down_flops,
                read + down_read,
            )
        else:
            out = call(
                functools.partial(down_kernel, index * step),
                "down",
                out_shape,
                [SMEM] + [VMEM] * 4,
                down_scratch,
                (place, hidden, shared_hidden, *down_weights),
                down_flops,
                down_read,
            )
        partials.append(out)

    results = []
    for keep_far, keep_near, send_far, send_near in partials:
        far = keep_far + swap(send_far, "local", 1).astype(f32)
        came = [swap(far[k].astype(bf16), "local", k * CORES) for k in range(1, pairs)]
        near = keep_near + swap(send_near, "local", 1).astype(f32)
        rows_shape = jax.ShapeDtypeStruct((tokens, step), bf16)
        near_shape = jax.ShapeDtypeStruct((half, tokens, step), bf16)
        out = call(
            relay_kernel,
            "relay",
            [rows_shape] * (node_count - half) + [near_shape] * (pairs - 1),
            [VMEM] * (pairs + 1),
            [],
            (far, near, *came),
        )
        far_rows, near_rows = out[: node_count - half], out[node_count - half :]
        near_came = [swap(x, "local", k * CORES).astype(f32) for k, x in enumerate(near_rows, 1)]
        far_came = [swap(x, "node", half + k).astype(f32) for k, x in enumerate(far_rows)]
        result = sum(near_came, near[0])
        total_here = result[0]
        for k in range(1, half):
            total_here = total_here + swap(result[k].astype(bf16), "node", k).astype(f32)
        total_here = sum(far_came, total_here)
        results.append(total_here)
    mixed = jnp.concatenate(results, axis=1)

    rows = jnp.stack(
        [lax.dynamic_slice(c, (me * tokens, 0), (tokens, depth)) for c in chunks]
    )
    bit = 1
    while bit < local_count:
        flipped = rows.reshape(local_count // (2 * bit), 2, bit, tokens, depth)[:, ::-1]
        rows = jnp.where((me & bit) != 0, flipped.reshape(rows.shape), rows)
        bit *= 2
    residual = rows.transpose(1, 0, 2).reshape(tokens, width).astype(jnp.float32)
    return (residual + mixed).astype(jnp.bfloat16)


def solution(mesh):
    in_specs = (
        P(("group", "node"), "local"),
        P(),
        P(("group", "node", "local"), None),
        P(("group", "node", "local"), None, None),
        P("node", None, "local"),
        P("node", None, "local"),
        P("node", "local", None),
        P(None, "local"),
        P(None, "local"),
        P("local", None),
    )
    out_specs = P(("group", "node", "local"), None)
    return jax.shard_map(
        on_device, mesh=mesh, in_specs=in_specs, out_specs=out_specs, check_vma=False
    )
```

```python
import functools

import jax
import jax.numpy as jnp
from jax import lax
from jax.experimental import pallas as pl
from jax.experimental.pallas import tpu as pltpu
from jax.sharding import PartitionSpec as P

ROWS = 128
LANES = 128
CORES = 2
WINDOW = 40
LATE = 2
VMEM = pl.BlockSpec(memory_space=pltpu.VMEM)
SMEM = pl.BlockSpec(memory_space=pltpu.SMEM)
ANY = pl.BlockSpec(memory_space=pl.ANY)
HBM = pl.BlockSpec(memory_space=pltpu.HBM)


def swap(x, axis, offset):
    size = lax.axis_size(axis)
    return lax.ppermute(x, axis, [(i, i ^ offset) for i in range(size)])


def in_hbm(x):
    return pltpu.with_memory_space_constraint(x, pltpu.HBM)


def row_loop(total, body):
    block = min(ROWS, total)
    if total == block:
        body(pl.ds(0, block))
        return

    @pl.loop(0, total // block)
    def _(index):
        body(pl.ds(pl.multiple_of(index * block, block), block))


def pack_kernel(pick, experts, place_ref, *refs):
    sources, (block_ref, gain_ref, rows_ref, ids_ref, gates_ref, sems) = refs[:4], refs[4:]
    own, depth = rows_ref.shape
    moves = [
        pltpu.make_async_copy(source, target, sems.at[index])
        for index, (source, target) in enumerate(zip(sources, (rows_ref, ids_ref, gates_ref, gain_ref)))
    ]
    for move in moves:
        move.start()
    for move in moves:
        move.wait()
    tokens = ids_ref.shape[1]
    diagonal = lax.broadcasted_iota(jnp.int32, (tokens, tokens), 0) == lax.broadcasted_iota(
        jnp.int32, (tokens, tokens), 1
    )
    lane = lax.broadcasted_iota(jnp.int32, (tokens, LANES), 1)
    tag = jnp.zeros((tokens, LANES), jnp.float32)
    for index in range(pick * (1 + experts)):
        ref, row = (ids_ref, index) if index < pick else (gates_ref, index - pick)
        values = ref[row : row + 1, :].astype(jnp.float32)
        column = jnp.sum(jnp.where(diagonal, values, 0.0), axis=1, keepdims=True)
        tag = jnp.where(lane == index, column, tag)
    tags = jnp.concatenate([tag] * (own // tokens), axis=0)
    row = lax.broadcasted_iota(jnp.int32, (own, LANES), 0)
    first = place_ref[0] * tokens
    mine = (row >= first) & (row < first + tokens)
    block_ref[:, :depth] = rows_ref[...]
    block_ref[:, depth:] = jnp.where(mine, tags, 0.0).astype(jnp.bfloat16)


class Queue:
    def __init__(self, moves):
        self.moves, self.waited = moves, 0
        for move in moves[:WINDOW]:
            move.start()

    def wait(self):
        self.moves[self.waited].wait()
        if self.waited + WINDOW < len(self.moves):
            self.moves[self.waited + WINDOW].start()
        self.waited += 1


def weight_moves(parts, weights, buffers, sems):
    gate, up, s_gate, s_up = weights
    buffer, shared_buffer = buffers
    experts, depth = gate.shape[0], buffer.shape[2]
    moves = []

    def move(source, target):
        moves.append(pltpu.make_async_copy(source, target, sems.at[len(moves)]))

    blocks = [pl.ds(pl.multiple_of(part * depth, depth), depth) for part in parts]
    for which, weight in enumerate((s_gate, s_up)):
        for index, rows in enumerate(blocks):
            move(weight.at[rows, :], shared_buffer.at[index, which])
    for slot in range(experts * 2):
        for index, rows in enumerate(blocks):
            move((gate, up)[slot % 2].at[slot // 2, rows, :], buffer.at[index, slot])
    return moves


def scaled_rows(chunk_ref, gain, rows):
    values = chunk_ref[rows, : gain.shape[1]].astype(jnp.float32)
    return values, (values * gain).astype(jnp.bfloat16)


def square_sums(chunk_ref, gain, lhs_ref, square_ref, square_in):
    def body(rows):
        values, lhs = scaled_rows(chunk_ref, gain, rows)
        lhs_ref[rows, :] = lhs
        square = jnp.sum(values * values, axis=1, keepdims=True)
        square = jnp.broadcast_to(square, (square.shape[0], LANES))
        square_ref[rows, :] = square if square_in is None else square + square_in[rows, :]

    row_loop(chunk_ref.shape[0], body)


def project_kernel(first, extra, part_ref, chunk_ref, gain_ref, *refs):
    weights, refs = refs[:4], refs[4 + extra :]
    (acc_in, shared_in, square_in), refs = ((None,) * 3, refs) if first else (refs[:3], refs[3:])
    acc_ref, shared_ref, square_ref, lhs_ref, buffer, shared_buffer, sems = refs
    part = part_ref[0]
    queue = Queue(weight_moves([part], weights, (buffer, shared_buffer), sems))
    square_sums(chunk_ref, gain_ref[part], lhs_ref, square_ref, square_in)
    inner, shared_inner = buffer.shape[3], shared_buffer.shape[3]
    own = shared_ref.shape[0]
    for which in range(2):
        queue.wait()
        columns = slice(which * shared_inner, (which + 1) * shared_inner)
        term = jnp.dot(
            lhs_ref[:own, :], shared_buffer[0, which], preferred_element_type=jnp.float32
        )
        shared_ref[:, columns] = term if first else term + shared_in[:, columns]
    for slot in range(buffer.shape[1]):
        queue.wait()
        columns = slice(slot * inner, (slot + 1) * inner)

        def body(rows):
            term = jnp.dot(lhs_ref[rows, :], buffer[0, slot], preferred_element_type=jnp.float32)
            acc_ref[rows, columns] = term if first else term + acc_in[rows, columns]

        row_loop(chunk_ref.shape[0], body)


def join_kernel(count, *refs):
    out_ref = refs[-1]
    start = 0
    for ref in refs[:count]:
        out_ref[start : start + ref.shape[0], :] = ref[...]
        start += ref.shape[0]


def relay_kernel(far_ref, *refs):
    pairs = far_ref.shape[0]
    for index, sum_ref in enumerate(refs[pairs - 1 :]):
        total = far_ref[0, index]
        for ref in refs[: pairs - 1]:
            total = total + ref[index].astype(jnp.float32)
        sum_ref[...] = total.astype(jnp.bfloat16)


def act(gate, up):
    return gate / (1.0 + jnp.exp(-gate)) * up


def row_share(tag, node, pick, experts, expert):
    share = jnp.zeros((tag.shape[0], 1), jnp.float32)
    for k in range(pick):
        column = pick + k * experts + expert
        share = share + jnp.where(
            tag[:, k : k + 1] == node.astype(jnp.float32), tag[:, column : column + 1], 0.0
        )
    return share


def row_blocks(total):
    block = min(ROWS, total)
    return [slice(start, start + block) for start in range(0, total, block)]


def down_expert(hidden_ref, shared_hidden_ref, expert, first, down, s_down, out_ref):
    inner = down.shape[1]
    count, _, step = out_ref.shape
    own = shared_hidden_ref.shape[0]
    for index in range(count):
        taken = slice(first + index * step, first + (index + 1) * step)
        for rows in row_blocks(hidden_ref.shape[0]):
            term = jnp.dot(
                hidden_ref[rows, expert * inner : (expert + 1) * inner],
                down[expert, :, taken],
                preferred_element_type=jnp.float32,
            )
            out_ref[index, rows, :] = term if expert == 0 else term + out_ref[index, rows, :]
        if expert == 0:
            out_ref[index, :own, :] += jnp.dot(
                shared_hidden_ref[...], s_down[:, taken], preferred_element_type=jnp.float32
            )


def leave(me, own, out_ref, outs):
    count, _, step = out_ref.shape
    keep_far, keep_near, send_far, send_near = outs
    pairs, near, tokens = keep_near.shape[:3]
    for index in range(count):
        columns = slice(index * step, (index + 1) * step)
        for pair in range(pairs):
            for side, to_refs in enumerate(((keep_near, keep_far), (send_near, send_far))):
                place = lax.bitwise_xor(me, pair * CORES + side) * tokens
                for other in range(near + keep_far.shape[1]):
                    rows = pl.ds(pl.multiple_of(other * own + place, tokens), tokens)
                    to_ref = to_refs[other >= near]
                    to_ref[pair, other % near, :, columns] = out_ref[index, rows, :].astype(to_ref.dtype)


def finish_kernel(
    width, pick, part_count, place_ref, gain_ref, gate, up, s_gate, s_up,
    acc_in, shared_in, square_in, down, s_down, *refs
):
    chunks, refs = refs[:part_count], refs[part_count:]
    (
        hidden_ref, shared_hidden_ref, *outs,
        lhs_ref, square_ref, share_ref, buffer, shared_buffer, out_ref, sems,
    ) = refs
    me, node = place_ref[0], place_ref[1]
    late = buffer.shape[0]
    parts = [lax.bitwise_xor(me, part_count - late + index) for index in range(late)]
    moves = weight_moves(parts, (gate, up, s_gate, s_up), (buffer, shared_buffer), sems)
    queue = Queue(moves)
    experts, inner, shared_inner = gate.shape[0], gate.shape[2], s_gate.shape[1]
    own, depth = shared_in.shape[0], gain_ref.shape[2]
    for index, part in enumerate(parts):
        square_sums(
            chunks[index - late], gain_ref[part], lhs_ref.at[index], square_ref,
            square_ref if index else square_in,
        )
    blocks = row_blocks(chunks[-1].shape[0])
    for rows in blocks:
        tag = sum(chunk[rows, depth:].astype(jnp.float32) for chunk in chunks)
        for expert in range(experts):
            share = row_share(tag, node, pick, experts, expert)
            share_ref[expert, rows, :] = jnp.broadcast_to(share, (share.shape[0], LANES))
        square_ref[rows, :] = lax.rsqrt(square_ref[rows, :] / width + 1e-06)

    def project(rows_list, before, weights):
        terms = [before[rows] for rows in rows_list]
        for index in range(late):
            queue.wait()
            for at, rows in enumerate(rows_list):
                terms[at] = terms[at] + jnp.dot(
                    lhs_ref[index, rows, :], weights(index), preferred_element_type=jnp.float32
                )
        return [term * square_ref[rows, :][:, :1] for term, rows in zip(terms, rows_list)]

    class Columns:
        def __init__(self, ref, start, count):
            self.ref, self.columns = ref, slice(start, start + count)

        def __getitem__(self, rows):
            return self.ref[rows, self.columns]

    projs = []
    for which in range(2):
        before = Columns(shared_in, which * shared_inner, shared_inner)
        projs += project([slice(0, own)], before, lambda index: shared_buffer[index, which])
    shared_hidden_ref[...] = act(*projs).astype(jnp.bfloat16)
    for expert in range(experts):
        projs = []
        for slot in (2 * expert, 2 * expert + 1):
            before = Columns(acc_in, slot * inner, inner)
            projs.append(project(blocks, before, lambda index: buffer[index, slot]))
        for rows, gate_proj, up_proj in zip(blocks, *projs):
            hidden_ref[rows, expert * inner : (expert + 1) * inner] = (
                act(gate_proj, up_proj) * share_ref[expert, rows, :][:, :1]
            ).astype(jnp.bfloat16)
        down_expert(hidden_ref, shared_hidden_ref, expert, 0, down, s_down, out_ref)
    leave(me, own, out_ref, outs)


def down_kernel(first, place_ref, hidden_ref, shared_hidden_ref, down, s_down, *refs):
    for expert in range(down.shape[0]):
        down_expert(hidden_ref, shared_hidden_ref, expert, first, down, s_down, refs[-1])
    leave(place_ref[0], shared_hidden_ref.shape[0], refs[-1], refs[:4])


def call(kernel, name, out_shape, in_specs, scratch, args, flops=0, read=0, aliases=None):
    held = [a for a, spec in zip(args, in_specs) if spec is VMEM and a.ndim < 3] + list(out_shape)
    held += [s for s in scratch if hasattr(s, "dtype") and s.memory_space == pltpu.VMEM]
    size = 0
    for array in held:
        count = jnp.dtype(array.dtype).itemsize
        for extent in array.shape:
            count *= extent
        size += count
    return pl.pallas_call(
        kernel,
        out_shape=out_shape,
        in_specs=in_specs,
        out_specs=[VMEM] * len(out_shape),
        scratch_shapes=scratch,
        input_output_aliases=aliases or {},
        compiler_params=pltpu.CompilerParams(vmem_limit_bytes=size + 8 * 2**20),
        cost_estimate=pl.CostEstimate(flops=flops, bytes_accessed=read, transcendentals=0),
        name=name,
    )(*args)


def on_device(attended, norm_gain, node_ids, gates, w_gate, w_up, w_down, s_gate, s_up, s_down):
    node_count = lax.axis_size("node")
    local_count = lax.axis_size("local")
    pairs = local_count // CORES
    node, me = lax.axis_index("node"), lax.axis_index("local")
    own, depth = attended.shape
    tokens, pick = node_ids.shape
    experts, width, inner = w_gate.shape
    shared_inner = s_gate.shape[1]
    total = node_count * own
    up_weights = tuple(in_hbm(w) for w in (w_gate, w_up, s_gate, s_up))
    down_weights = (w_down, s_down)
    f32, bf16 = jnp.float32, jnp.bfloat16

    inputs = (
        in_hbm(attended),
        in_hbm(node_ids.T),
        in_hbm(gates.transpose(1, 2, 0).reshape(pick * experts, tokens)),
        in_hbm(norm_gain.reshape(local_count, 1, depth)),
    )
    block, gain = call(
        functools.partial(pack_kernel, pick, experts),
        "pack",
        [
            jax.ShapeDtypeStruct((own, depth + LANES), bf16),
            jax.ShapeDtypeStruct((local_count, 1, depth), f32),
        ],
        [SMEM] + [HBM] * 4,
        [pltpu.VMEM(x.shape, x.dtype) for x in inputs[:3]] + [pltpu.SemaphoreType.DMA((4,))],
        (me[None], *inputs),
        flops=4 * 10**10,
    )
    blocks = [block] + [swap(block, "node", k) for k in range(1, node_count)]
    rest = jnp.concatenate(blocks[1:], axis=0)
    column = jnp.concatenate([block, rest], axis=0)
    chunks = [column, swap(column, "local", 1)]

    def neighbour(k, sums):
        (column,) = call(
            functools.partial(join_kernel, 2),
            "join",
            [jax.ShapeDtypeStruct(chunks[0].shape, bf16)],
            [VMEM, VMEM, ANY],
            [],
            (first_rows[k - 1], other_rows[k - 1], sums[2]),
        )
        return [column, swap(column, "local", 1)]

    first_rows = [swap(block, "local", k * CORES) for k in range(1, pairs)]
    other_rows = [swap(rest, "local", k * CORES) for k in range(1, pairs)]

    sums_shape = [
        jax.ShapeDtypeStruct((total, experts * 2 * inner), f32),
        jax.ShapeDtypeStruct((own, 2 * shared_inner), f32),
        jax.ShapeDtypeStruct((total, LANES), f32),
    ]
    flops = 2 * depth * (total * experts * 2 * inner + own * 2 * shared_inner)
    read = 2 * depth * (experts * 2 * inner + 2 * shared_inner)
    weight_scratch = [
        pltpu.VMEM((1, experts * 2, depth, inner), bf16),
        pltpu.VMEM((1, 2, depth, shared_inner), bf16),
    ]
    lhs_scratch = pltpu.VMEM((total, depth), bf16)
    moves = experts * 2 + 2
    sums = None
    for offset in range(local_count - LATE):
        first = sums is None
        if offset == CORES - 1:
            for k in range(1, pairs):
                chunks += neighbour(k, sums)
        args = (lax.bitwise_xor(me, offset)[None], chunks[offset], gain, *up_weights)
        more = tuple(first_rows) if first else tuple(sums)
        sums = call(
            functools.partial(project_kernel, first, len(more) if first else 0),
            "project",
            sums_shape,
            [SMEM, VMEM, VMEM] + [HBM] * 4 + [ANY if first else VMEM] * len(more),
            [lhs_scratch, *weight_scratch, pltpu.SemaphoreType.DMA((moves,))],
            args + more,
            flops,
            read,
            aliases={} if first else {7: 0, 8: 1, 9: 2},
        )
    place = jnp.stack([me, node])

    slices = max(1, total // ROWS)
    step = width // slices
    half = node_count // 2
    out_shape = [
        jax.ShapeDtypeStruct((pairs, half, tokens, step), dtype)
        for dtype in (f32, f32, bf16, bf16)
    ]
    pieces = max(1, step // (10 * LANES))
    down_scratch = [
        pltpu.VMEM((pieces, total, step // pieces), f32),
    ]
    down_flops = 2 * step * (total * experts * inner + own * shared_inner)
    down_read = 2 * step * (experts * inner + shared_inner)
    partials = []
    for index in range(slices):
        if index == 0:
            hidden, shared_hidden, *out = call(
                functools.partial(finish_kernel, width, pick, local_count),
                "finish",
                [
                    jax.ShapeDtypeStruct((total, experts * inner), bf16),
                    jax.ShapeDtypeStruct((own, shared_inner), bf16),
                ]
                + out_shape,
                [SMEM, VMEM] + [HBM] * 4 + [VMEM] * (5 + local_count),
                [
                    pltpu.VMEM((LATE, total, depth), bf16),
                    pltpu.VMEM((total, LANES), f32),
                    pltpu.VMEM((experts, total, LANES), f32),
                    *(pltpu.VMEM((LATE, *w.shape[1:]), bf16) for w in weight_scratch),
                    *down_scratch,
                    pltpu.SemaphoreType.DMA((LATE * moves,)),
                ],
                (place, gain, *up_weights, *sums, *down_weights, *chunks),
                flops + down_flops,
                read + down_read,
            )
        else:
            out = call(
                functools.partial(down_kernel, index * step),
                "down",
                out_shape,
                [SMEM] + [VMEM] * 4,
                down_scratch,
                (place, hidden, shared_hidden, *down_weights),
                down_flops,
                down_read,
            )
        partials.append(out)

    results = []
    for keep_far, keep_near, send_far, send_near in partials:
        far = keep_far + swap(send_far, "local", 1).astype(f32)
        came = [swap(far[k].astype(bf16), "local", k * CORES) for k in range(1, pairs)]
        near = keep_near + swap(send_near, "local", 1).astype(f32)
        near_came = [
            swap(near[k].astype(bf16), "local", k * CORES).astype(f32) for k in range(1, pairs)
        ]
        far_rows = call(
            relay_kernel,
            "relay",
            [jax.ShapeDtypeStruct((tokens, step), bf16)] * (node_count - half),
            [VMEM] * pairs,
            [],
            (far, *came),
        )
        far_came = [swap(x, "node", half + k).astype(f32) for k, x in enumerate(far_rows)]
        result = sum(near_came, near[0])
        total_here = result[0]
        for k in range(1, half):
            total_here = total_here + swap(result[k].astype(bf16), "node", k).astype(f32)
        total_here = sum(far_came, total_here)
        results.append(total_here)
    mixed = jnp.concatenate(results, axis=1)

    rows = jnp.stack(
        [lax.dynamic_slice(c, (me * tokens, 0), (tokens, depth)) for c in chunks]
    )
    bit = 1
    while bit < local_count:
        flipped = rows.reshape(local_count // (2 * bit), 2, bit, tokens, depth)[:, ::-1]
        rows = jnp.where((me & bit) != 0, flipped.reshape(rows.shape), rows)
        bit *= 2
    residual = rows.transpose(1, 0, 2).reshape(tokens, width).astype(jnp.float32)
    return (residual + mixed).astype(jnp.bfloat16)


def solution(mesh):
    in_specs = (
        P(("group", "node"), "local"),
        P(),
        P(("group", "node", "local"), None),
        P(("group", "node", "local"), None, None),
        P("node", None, "local"),
        P("node", None, "local"),
        P("node", "local", None),
        P(None, "local"),
        P(None, "local"),
        P("local", None),
    )
    out_specs = P(("group", "node", "local"), None)
    return jax.shard_map(
        on_device, mesh=mesh, in_specs=in_specs, out_specs=out_specs, check_vma=False
    )
```

```python
import functools

import jax
import jax.numpy as jnp
from jax import lax
from jax.experimental import pallas as pl
from jax.experimental.pallas import tpu as pltpu
from jax.sharding import PartitionSpec as P

ROWS = 128
LANES = 128
CORES = 2
WINDOW = 9
LATE = 2
VMEM = pl.BlockSpec(memory_space=pltpu.VMEM)
SMEM = pl.BlockSpec(memory_space=pltpu.SMEM)
ANY = pl.BlockSpec(memory_space=pl.ANY)
HBM = pl.BlockSpec(memory_space=pltpu.HBM)


def swap(x, axis, offset):
    size = lax.axis_size(axis)
    return lax.ppermute(x, axis, [(i, i ^ offset) for i in range(size)])


def in_hbm(x):
    return pltpu.with_memory_space_constraint(x, pltpu.HBM)


def row_loop(total, body):
    block = min(ROWS, total)
    if total == block:
        body(pl.ds(0, block))
        return

    @pl.loop(0, total // block)
    def _(index):
        body(pl.ds(pl.multiple_of(index * block, block), block))


def pack_kernel(pick, experts, place_ref, *refs):
    sources, (block_ref, gain_ref, rows_ref, ids_ref, gates_ref, sems) = refs[:4], refs[4:]
    own, depth = rows_ref.shape
    moves = [
        pltpu.make_async_copy(source, target, sems.at[index])
        for index, (source, target) in enumerate(zip(sources, (rows_ref, ids_ref, gates_ref, gain_ref)))
    ]
    for move in moves:
        move.start()
    for move in moves:
        move.wait()
    tokens = ids_ref.shape[1]
    diagonal = lax.broadcasted_iota(jnp.int32, (tokens, tokens), 0) == lax.broadcasted_iota(
        jnp.int32, (tokens, tokens), 1
    )
    lane = lax.broadcasted_iota(jnp.int32, (tokens, LANES), 1)
    tag = jnp.zeros((tokens, LANES), jnp.float32)
    for index in range(pick * (1 + experts)):
        ref, row = (ids_ref, index) if index < pick else (gates_ref, index - pick)
        values = ref[row : row + 1, :].astype(jnp.float32)
        column = jnp.sum(jnp.where(diagonal, values, 0.0), axis=1, keepdims=True)
        tag = jnp.where(lane == index, column, tag)
    tags = jnp.concatenate([tag] * (own // tokens), axis=0)
    row = lax.broadcasted_iota(jnp.int32, (own, LANES), 0)
    first = place_ref[0] * tokens
    mine = (row >= first) & (row < first + tokens)
    block_ref[:, :depth] = rows_ref[...]
    block_ref[:, depth:] = jnp.where(mine, tags, 0.0).astype(jnp.bfloat16)


class Queue:
    def __init__(self, moves):
        self.moves, self.waited = moves, 0
        for move in moves[:WINDOW]:
            move.start()

    def wait(self):
        self.moves[self.waited].wait()
        if self.waited + WINDOW < len(self.moves):
            self.moves[self.waited + WINDOW].start()
        self.waited += 1


def weight_moves(parts, weights, buffers, sems):
    gate, up, s_gate, s_up = weights
    buffer, shared_buffer = buffers
    experts, depth = gate.shape[0], buffer.shape[2]
    moves = []

    def move(source, target):
        moves.append(pltpu.make_async_copy(source, target, sems.at[len(moves)]))

    blocks = [pl.ds(pl.multiple_of(part * depth, depth), depth) for part in parts]
    for which, weight in enumerate((s_gate, s_up)):
        for index, rows in enumerate(blocks):
            move(weight.at[rows, :], shared_buffer.at[index, which])
    for slot in range(experts * 2):
        for index, rows in enumerate(blocks):
            move((gate, up)[slot % 2].at[slot // 2, rows, :], buffer.at[index, slot])
    return moves


def scaled_rows(chunk_ref, gain, rows):
    values = chunk_ref[rows, : gain.shape[1]].astype(jnp.float32)
    return values, (values * gain).astype(jnp.bfloat16)


def square_sums(chunk_ref, gain, lhs_ref, square_ref, square_in):
    def body(rows):
        values, lhs = scaled_rows(chunk_ref, gain, rows)
        lhs_ref[rows, :] = lhs
        square = jnp.sum(values * values, axis=1, keepdims=True)
        square = jnp.broadcast_to(square, (square.shape[0], LANES))
        square_ref[rows, :] = square if square_in is None else square + square_in[rows, :]

    row_loop(chunk_ref.shape[0], body)


def project_kernel(first, extra, part_ref, chunk_ref, gain_ref, *refs):
    weights, refs = refs[:4], refs[4 + extra :]
    (acc_in, shared_in, square_in), refs = ((None,) * 3, refs) if first else (refs[:3], refs[3:])
    acc_ref, shared_ref, square_ref, lhs_ref, buffer, shared_buffer, sems = refs
    part = part_ref[0]
    queue = Queue(weight_moves([part], weights, (buffer, shared_buffer), sems))
    square_sums(chunk_ref, gain_ref[part], lhs_ref, square_ref, square_in)
    inner, shared_inner = buffer.shape[3], shared_buffer.shape[3]
    own = shared_ref.shape[0]
    for which in range(2):
        queue.wait()
        columns = slice(which * shared_inner, (which + 1) * shared_inner)
        term = jnp.dot(
            lhs_ref[:own, :], shared_buffer[0, which], preferred_element_type=jnp.float32
        )
        shared_ref[:, columns] = term if first else term + shared_in[:, columns]
    for slot in range(buffer.shape[1]):
        queue.wait()
        columns = slice(slot * inner, (slot + 1) * inner)

        def body(rows):
            term = jnp.dot(lhs_ref[rows, :], buffer[0, slot], preferred_element_type=jnp.float32)
            acc_ref[rows, columns] = term if first else term + acc_in[rows, columns]

        row_loop(chunk_ref.shape[0], body)


def join_kernel(count, *refs):
    out_ref = refs[-1]
    start = 0
    for ref in refs[:count]:
        out_ref[start : start + ref.shape[0], :] = ref[...]
        start += ref.shape[0]


def relay_kernel(far_ref, *refs):
    pairs = far_ref.shape[0]
    for index, sum_ref in enumerate(refs[pairs - 1 :]):
        total = far_ref[0, index]
        for ref in refs[: pairs - 1]:
            total = total + ref[index].astype(jnp.float32)
        sum_ref[...] = total.astype(jnp.bfloat16)


def act(gate, up):
    return gate / (1.0 + jnp.exp(-gate)) * up


def row_share(tag, node, pick, experts, expert):
    share = jnp.zeros((tag.shape[0], 1), jnp.float32)
    for k in range(pick):
        column = pick + k * experts + expert
        share = share + jnp.where(
            tag[:, k : k + 1] == node.astype(jnp.float32), tag[:, column : column + 1], 0.0
        )
    return share


def row_blocks(total):
    block = min(ROWS, total)
    return [slice(start, start + block) for start in range(0, total, block)]


def down_shared(shared_hidden_ref, first, s_down, out_ref):
    count, _, step = out_ref.shape
    own = shared_hidden_ref.shape[0]
    for index in range(count):
        taken = slice(first + index * step, first + (index + 1) * step)
        out_ref[index, :own, :] += jnp.dot(
            shared_hidden_ref[...], s_down[:, taken], preferred_element_type=jnp.float32
        )


def down_expert(hidden_ref, expert, first, down, out_ref):
    inner = down.shape[1]
    count, _, step = out_ref.shape
    for index in range(count):
        taken = slice(first + index * step, first + (index + 1) * step)
        for rows in row_blocks(hidden_ref.shape[0]):
            term = jnp.dot(
                hidden_ref[rows, expert * inner : (expert + 1) * inner],
                down[expert, :, taken],
                preferred_element_type=jnp.float32,
            )
            out_ref[index, rows, :] = term if expert == 0 else term + out_ref[index, rows, :]


def leave(me, own, out_ref, outs):
    count, _, step = out_ref.shape
    keep_far, keep_near, send_far, send_near = outs
    pairs, near, tokens = keep_near.shape[:3]
    for index in range(count):
        columns = slice(index * step, (index + 1) * step)
        for pair in range(pairs):
            for side, to_refs in enumerate(((keep_near, keep_far), (send_near, send_far))):
                place = lax.bitwise_xor(me, pair * CORES + side) * tokens
                for other in range(near + keep_far.shape[1]):
                    rows = pl.ds(pl.multiple_of(other * own + place, tokens), tokens)
                    to_ref = to_refs[other >= near]
                    to_ref[pair, other % near, :, columns] = out_ref[index, rows, :].astype(to_ref.dtype)


def finish_kernel(
    width, pick, part_count, place_ref, gain_ref, gate, up, s_gate, s_up,
    acc_in, shared_in, square_in, down, s_down, *refs
):
    chunks, refs = refs[:part_count], refs[part_count:]
    (
        hidden_ref, shared_hidden_ref, *outs,
        lhs_ref, square_ref, share_ref, buffer, shared_buffer, s_down_buffer, out_ref, sems,
    ) = refs
    me, node = place_ref[0], place_ref[1]
    late = buffer.shape[0]
    parts = [lax.bitwise_xor(me, part_count - late + index) for index in range(late)]
    moves = weight_moves(parts, (gate, up, s_gate, s_up), (buffer, shared_buffer), sems)
    moves.append(pltpu.make_async_copy(s_down, s_down_buffer, sems.at[len(moves)]))
    queue = Queue(moves)
    experts, inner, shared_inner = gate.shape[0], gate.shape[2], s_gate.shape[1]
    own, depth = shared_in.shape[0], gain_ref.shape[2]
    for index, part in enumerate(parts):
        square_sums(
            chunks[index - late], gain_ref[part], lhs_ref.at[index], square_ref,
            square_ref if index else square_in,
        )
    blocks = row_blocks(chunks[-1].shape[0])
    for rows in blocks:
        tag = sum(chunk[rows, depth:].astype(jnp.float32) for chunk in chunks)
        for expert in range(experts):
            share = row_share(tag, node, pick, experts, expert)
            share_ref[expert, rows, :] = jnp.broadcast_to(share, (share.shape[0], LANES))
        square_ref[rows, :] = lax.rsqrt(square_ref[rows, :] / width + 1e-06)

    def project(rows_list, before, weights):
        terms = [before[rows] for rows in rows_list]
        for index in range(late):
            queue.wait()
            for at, rows in enumerate(rows_list):
                terms[at] = terms[at] + jnp.dot(
                    lhs_ref[index, rows, :], weights(index), preferred_element_type=jnp.float32
                )
        return [term * square_ref[rows, :][:, :1] for term, rows in zip(terms, rows_list)]

    class Columns:
        def __init__(self, ref, start, count):
            self.ref, self.columns = ref, slice(start, start + count)

        def __getitem__(self, rows):
            return self.ref[rows, self.columns]

    projs = []
    for which in range(2):
        before = Columns(shared_in, which * shared_inner, shared_inner)
        projs += project([slice(0, own)], before, lambda index: shared_buffer[index, which])
    shared_hidden_ref[...] = act(*projs).astype(jnp.bfloat16)
    for expert in range(experts):
        projs = []
        for slot in (2 * expert, 2 * expert + 1):
            before = Columns(acc_in, slot * inner, inner)
            projs.append(project(blocks, before, lambda index: buffer[index, slot]))
        for rows, gate_proj, up_proj in zip(blocks, *projs):
            hidden_ref[rows, expert * inner : (expert + 1) * inner] = (
                act(gate_proj, up_proj) * share_ref[expert, rows, :][:, :1]
            ).astype(jnp.bfloat16)
        down_expert(hidden_ref, expert, 0, down, out_ref)
    queue.wait()
    down_shared(shared_hidden_ref, 0, s_down_buffer, out_ref)
    leave(me, own, out_ref, outs)


def down_kernel(first, place_ref, hidden_ref, shared_hidden_ref, down, s_down, *refs):
    for expert in range(down.shape[0]):
        down_expert(hidden_ref, expert, first, down, refs[-1])
    down_shared(shared_hidden_ref, first, s_down, refs[-1])
    leave(place_ref[0], shared_hidden_ref.shape[0], refs[-1], refs[:4])


def call(kernel, name, out_shape, in_specs, scratch, args, flops=0, read=0, aliases=None):
    held = [a for a, spec in zip(args, in_specs) if spec is VMEM and a.ndim < 3] + list(out_shape)
    held += [s for s in scratch if hasattr(s, "dtype") and s.memory_space == pltpu.VMEM]
    size = 0
    for array in held:
        count = jnp.dtype(array.dtype).itemsize
        for extent in array.shape:
            count *= extent
        size += count
    return pl.pallas_call(
        kernel,
        out_shape=out_shape,
        in_specs=in_specs,
        out_specs=[VMEM] * len(out_shape),
        scratch_shapes=scratch,
        input_output_aliases=aliases or {},
        compiler_params=pltpu.CompilerParams(vmem_limit_bytes=size + 8 * 2**20),
        cost_estimate=pl.CostEstimate(flops=flops, bytes_accessed=read, transcendentals=0),
        name=name,
    )(*args)


def on_device(attended, norm_gain, node_ids, gates, w_gate, w_up, w_down, s_gate, s_up, s_down):
    node_count = lax.axis_size("node")
    local_count = lax.axis_size("local")
    pairs = local_count // CORES
    node, me = lax.axis_index("node"), lax.axis_index("local")
    own, depth = attended.shape
    tokens, pick = node_ids.shape
    experts, width, inner = w_gate.shape
    shared_inner = s_gate.shape[1]
    total = node_count * own
    up_weights = tuple(in_hbm(w) for w in (w_gate, w_up, s_gate, s_up))
    down_weights = (w_down, s_down)
    f32, bf16 = jnp.float32, jnp.bfloat16

    inputs = (
        in_hbm(attended),
        in_hbm(node_ids.T),
        in_hbm(gates.transpose(1, 2, 0).reshape(pick * experts, tokens)),
        in_hbm(norm_gain.reshape(local_count, 1, depth)),
    )
    block, gain = call(
        functools.partial(pack_kernel, pick, experts),
        "pack",
        [
            jax.ShapeDtypeStruct((own, depth + LANES), bf16),
            jax.ShapeDtypeStruct((local_count, 1, depth), f32),
        ],
        [SMEM] + [HBM] * 4,
        [pltpu.VMEM(x.shape, x.dtype) for x in inputs[:3]] + [pltpu.SemaphoreType.DMA((4,))],
        (me[None], *inputs),
        flops=4 * 10**10,
    )
    blocks = [block] + [swap(block, "node", k) for k in range(1, node_count)]
    rest = jnp.concatenate(blocks[1:], axis=0)
    column = jnp.concatenate([block, rest], axis=0)
    chunks = [column, swap(column, "local", 1)]

    def neighbour(k, sums):
        (column,) = call(
            functools.partial(join_kernel, 2),
            "join",
            [jax.ShapeDtypeStruct(chunks[0].shape, bf16)],
            [VMEM, VMEM, ANY],
            [],
            (first_rows[k - 1], other_rows[k - 1], sums[2]),
        )
        return [column, swap(column, "local", 1)]

    first_rows = [swap(block, "local", k * CORES) for k in range(1, pairs)]
    other_rows = [swap(rest, "local", k * CORES) for k in range(1, pairs)]

    sums_shape = [
        jax.ShapeDtypeStruct((total, experts * 2 * inner), f32),
        jax.ShapeDtypeStruct((own, 2 * shared_inner), f32),
        jax.ShapeDtypeStruct((total, LANES), f32),
    ]
    flops = 2 * depth * (total * experts * 2 * inner + own * 2 * shared_inner)
    read = 2 * depth * (experts * 2 * inner + 2 * shared_inner)
    weight_scratch = [
        pltpu.VMEM((1, experts * 2, depth, inner), bf16),
        pltpu.VMEM((1, 2, depth, shared_inner), bf16),
    ]
    lhs_scratch = pltpu.VMEM((total, depth), bf16)
    moves = experts * 2 + 2
    sums = None
    for offset in range(local_count - LATE):
        first = sums is None
        if offset == CORES - 1:
            for k in range(1, pairs):
                chunks += neighbour(k, sums)
        args = (lax.bitwise_xor(me, offset)[None], chunks[offset], gain, *up_weights)
        more = tuple(first_rows) if first else tuple(sums)
        sums = call(
            functools.partial(project_kernel, first, len(more) if first else 0),
            "project",
            sums_shape,
            [SMEM, VMEM, VMEM] + [HBM] * 4 + [ANY if first else VMEM] * len(more),
            [lhs_scratch, *weight_scratch, pltpu.SemaphoreType.DMA((moves,))],
            args + more,
            flops,
            read,
            aliases={} if first else {7: 0, 8: 1, 9: 2},
        )
    place = jnp.stack([me, node])

    slices = max(1, total // ROWS)
    step = width // slices
    half = node_count // 2
    out_shape = [
        jax.ShapeDtypeStruct((pairs, half, tokens, step), dtype)
        for dtype in (f32, f32, bf16, bf16)
    ]
    pieces = max(1, step // (10 * LANES))
    down_scratch = [
        pltpu.VMEM((pieces, total, step // pieces), f32),
    ]
    down_flops = 2 * step * (total * experts * inner + own * shared_inner)
    down_read = 2 * step * (experts * inner + shared_inner)
    partials = []
    for index in range(slices):
        if index == 0:
            hidden, shared_hidden, *out = call(
                functools.partial(finish_kernel, width, pick, local_count),
                "finish",
                [
                    jax.ShapeDtypeStruct((total, experts * inner), bf16),
                    jax.ShapeDtypeStruct((own, shared_inner), bf16),
                ]
                + out_shape,
                [SMEM, VMEM] + [HBM] * 4 + [VMEM] * 4 + [HBM] + [VMEM] * local_count,
                [
                    pltpu.VMEM((LATE, total, depth), bf16),
                    pltpu.VMEM((total, LANES), f32),
                    pltpu.VMEM((experts, total, LANES), f32),
                    *(pltpu.VMEM((LATE, *w.shape[1:]), bf16) for w in weight_scratch),
                    pltpu.VMEM(s_down.shape, bf16),
                    *down_scratch,
                    pltpu.SemaphoreType.DMA((LATE * moves + 1,)),
                ],
                (place, gain, *up_weights, *sums, w_down, in_hbm(s_down), *chunks),
                flops + down_flops,
                read + down_read,
            )
        else:
            out = call(
                functools.partial(down_kernel, index * step),
                "down",
                out_shape,
                [SMEM] + [VMEM] * 4,
                down_scratch,
                (place, hidden, shared_hidden, *down_weights),
                down_flops,
                down_read,
            )
        partials.append(out)

    results = []
    for keep_far, keep_near, send_far, send_near in partials:
        far = keep_far + swap(send_far, "local", 1).astype(f32)
        came = [swap(far[k].astype(bf16), "local", k * CORES) for k in range(1, pairs)]
        near = keep_near + swap(send_near, "local", 1).astype(f32)
        near_came = [
            swap(near[k].astype(bf16), "local", k * CORES).astype(f32) for k in range(1, pairs)
        ]
        far_rows = call(
            relay_kernel,
            "relay",
            [jax.ShapeDtypeStruct((tokens, step), bf16)] * (node_count - half),
            [VMEM] * pairs,
            [],
            (far, *came),
        )
        far_came = [swap(x, "node", half + k).astype(f32) for k, x in enumerate(far_rows)]
        result = sum(near_came, near[0])
        total_here = result[0]
        for k in range(1, half):
            total_here = total_here + swap(result[k].astype(bf16), "node", k).astype(f32)
        total_here = sum(far_came, total_here)
        results.append(total_here)
    mixed = jnp.concatenate(results, axis=1)

    rows = jnp.stack(
        [lax.dynamic_slice(c, (me * tokens, 0), (tokens, depth)) for c in chunks]
    )
    bit = 1
    while bit < local_count:
        flipped = rows.reshape(local_count // (2 * bit), 2, bit, tokens, depth)[:, ::-1]
        rows = jnp.where((me & bit) != 0, flipped.reshape(rows.shape), rows)
        bit *= 2
    residual = rows.transpose(1, 0, 2).reshape(tokens, width).astype(jnp.float32)
    return (residual + mixed).astype(jnp.bfloat16)


def solution(mesh):
    in_specs = (
        P(("group", "node"), "local"),
        P(),
        P(("group", "node", "local"), None),
        P(("group", "node", "local"), None, None),
        P("node", None, "local"),
        P("node", None, "local"),
        P("node", "local", None),
        P(None, "local"),
        P(None, "local"),
        P("local", None),
    )
    out_specs = P(("group", "node", "local"), None)
    return jax.shard_map(
        on_device, mesh=mesh, in_specs=in_specs, out_specs=out_specs, check_vma=False
    )
```

```python
import functools

import jax
import jax.numpy as jnp
from jax import lax
from jax.experimental import pallas as pl
from jax.experimental.pallas import tpu as pltpu
from jax.sharding import PartitionSpec as P

ROWS = 128
LANES = 128
CORES = 2
WINDOW = 9
LATE = 2
VMEM = pl.BlockSpec(memory_space=pltpu.VMEM)
SMEM = pl.BlockSpec(memory_space=pltpu.SMEM)
ANY = pl.BlockSpec(memory_space=pl.ANY)
HBM = pl.BlockSpec(memory_space=pltpu.HBM)


def swap(x, axis, offset):
    size = lax.axis_size(axis)
    return lax.ppermute(x, axis, [(i, i ^ offset) for i in range(size)])


def in_hbm(x):
    return pltpu.with_memory_space_constraint(x, pltpu.HBM)


def row_loop(total, body):
    block = min(ROWS, total)
    if total == block:
        body(pl.ds(0, block))
        return

    @pl.loop(0, total // block)
    def _(index):
        body(pl.ds(pl.multiple_of(index * block, block), block))


def pack_kernel(pick, experts, place_ref, *refs):
    sources, (block_ref, gain_ref, rows_ref, ids_ref, gates_ref, sems) = refs[:4], refs[4:]
    own, depth = rows_ref.shape
    moves = [
        pltpu.make_async_copy(source, target, sems.at[index])
        for index, (source, target) in enumerate(zip(sources, (rows_ref, ids_ref, gates_ref, gain_ref)))
    ]
    for move in moves:
        move.start()
    for move in moves:
        move.wait()
    tokens = ids_ref.shape[1]
    diagonal = lax.broadcasted_iota(jnp.int32, (tokens, tokens), 0) == lax.broadcasted_iota(
        jnp.int32, (tokens, tokens), 1
    )
    lane = lax.broadcasted_iota(jnp.int32, (tokens, LANES), 1)
    tag = jnp.zeros((tokens, LANES), jnp.float32)
    for index in range(pick * (1 + experts)):
        ref, row = (ids_ref, index) if index < pick else (gates_ref, index - pick)
        values = ref[row : row + 1, :].astype(jnp.float32)
        column = jnp.sum(jnp.where(diagonal, values, 0.0), axis=1, keepdims=True)
        tag = jnp.where(lane == index, column, tag)
    tags = jnp.concatenate([tag] * (own // tokens), axis=0)
    row = lax.broadcasted_iota(jnp.int32, (own, LANES), 0)
    first = place_ref[0] * tokens
    mine = (row >= first) & (row < first + tokens)
    block_ref[:, :depth] = rows_ref[...]
    block_ref[:, depth:] = jnp.where(mine, tags, 0.0).astype(jnp.bfloat16)


class Queue:
    def __init__(self, moves):
        self.moves, self.waited = moves, 0
        for move in moves[:WINDOW]:
            move.start()

    def wait(self):
        self.moves[self.waited].wait()
        if self.waited + WINDOW < len(self.moves):
            self.moves[self.waited + WINDOW].start()
        self.waited += 1


def weight_moves(parts, weights, buffers, sems):
    gate, up, s_gate, s_up = weights
    buffer, shared_buffer = buffers
    experts, depth = gate.shape[0], buffer.shape[2]
    moves = []

    def move(source, target):
        moves.append(pltpu.make_async_copy(source, target, sems.at[len(moves)]))

    blocks = [pl.ds(pl.multiple_of(part * depth, depth), depth) for part in parts]
    for which, weight in enumerate((s_gate, s_up)):
        for index, rows in enumerate(blocks):
            move(weight.at[rows, :], shared_buffer.at[index, which])
    for slot in range(experts * 2):
        for index, rows in enumerate(blocks):
            move((gate, up)[slot % 2].at[slot // 2, rows, :], buffer.at[index, slot])
    return moves


def scaled_rows(chunk_ref, gain, rows):
    values = chunk_ref[rows, : gain.shape[1]].astype(jnp.float32)
    return values, (values * gain).astype(jnp.bfloat16)


def square_sums(chunk_ref, gain, lhs_ref, square_ref, square_in):
    def body(rows):
        values, lhs = scaled_rows(chunk_ref, gain, rows)
        lhs_ref[rows, :] = lhs
        square = jnp.sum(values * values, axis=1, keepdims=True)
        square = jnp.broadcast_to(square, (square.shape[0], LANES))
        square_ref[rows, :] = square if square_in is None else square + square_in[rows, :]

    row_loop(chunk_ref.shape[0], body)


def project_kernel(first, extra, part_ref, chunk_ref, gain_ref, *refs):
    weights, refs = refs[:4], refs[4 + extra :]
    (acc_in, shared_in, square_in), refs = ((None,) * 3, refs) if first else (refs[:3], refs[3:])
    acc_ref, shared_ref, square_ref, lhs_ref, buffer, shared_buffer, sems = refs
    part = part_ref[0]
    queue = Queue(weight_moves([part], weights, (buffer, shared_buffer), sems))
    square_sums(chunk_ref, gain_ref[part], lhs_ref, square_ref, square_in)
    inner, shared_inner = buffer.shape[3], shared_buffer.shape[3]
    own = shared_ref.shape[0]
    for which in range(2):
        queue.wait()
        columns = slice(which * shared_inner, (which + 1) * shared_inner)
        term = jnp.dot(
            lhs_ref[:own, :], shared_buffer[0, which], preferred_element_type=jnp.float32
        )
        shared_ref[:, columns] = term if first else term + shared_in[:, columns]
    for slot in range(buffer.shape[1]):
        queue.wait()
        columns = slice(slot * inner, (slot + 1) * inner)

        def body(rows):
            term = jnp.dot(lhs_ref[rows, :], buffer[0, slot], preferred_element_type=jnp.float32)
            acc_ref[rows, columns] = term if first else term + acc_in[rows, columns]

        row_loop(chunk_ref.shape[0], body)


def join_kernel(count, *refs):
    out_ref = refs[-1]
    start = 0
    for ref in refs[:count]:
        out_ref[start : start + ref.shape[0], :] = ref[...]
        start += ref.shape[0]


def relay_kernel(far_ref, *refs):
    pairs = far_ref.shape[0]
    for index, sum_ref in enumerate(refs[pairs - 1 :]):
        total = far_ref[0, index]
        for ref in refs[: pairs - 1]:
            total = total + ref[index].astype(jnp.float32)
        sum_ref[...] = total.astype(jnp.bfloat16)


def act(gate, up):
    return gate / (1.0 + jnp.exp(-gate)) * up


def row_share(tag, node, pick, experts, expert):
    share = jnp.zeros((tag.shape[0], 1), jnp.float32)
    for k in range(pick):
        column = pick + k * experts + expert
        share = share + jnp.where(
            tag[:, k : k + 1] == node.astype(jnp.float32), tag[:, column : column + 1], 0.0
        )
    return share


def row_blocks(total):
    block = min(ROWS, total)
    return [slice(start, start + block) for start in range(0, total, block)]


def down_shared(shared_hidden_ref, first, s_down, out_ref, pieces):
    step = out_ref.shape[2]
    own = shared_hidden_ref.shape[0]
    for index in pieces:
        taken = slice(first + index * step, first + (index + 1) * step)
        out_ref[index, :own, :] += jnp.dot(
            shared_hidden_ref[...], s_down[:, taken], preferred_element_type=jnp.float32
        )


def down_expert(hidden_ref, expert, first, down, out_ref, pieces):
    inner = down.shape[1]
    step = out_ref.shape[2]
    for index in pieces:
        taken = slice(first + index * step, first + (index + 1) * step)
        for rows in row_blocks(hidden_ref.shape[0]):
            term = jnp.dot(
                hidden_ref[rows, expert * inner : (expert + 1) * inner],
                down[expert, :, taken],
                preferred_element_type=jnp.float32,
            )
            out_ref[index, rows, :] = term if expert == 0 else term + out_ref[index, rows, :]


def leave(me, own, out_ref, outs, pieces):
    step = out_ref.shape[2]
    keep_far, keep_near, send_far, send_near = outs
    pairs, near, tokens = keep_near.shape[:3]
    for index in pieces:
        columns = slice(index * step, (index + 1) * step)
        for pair in range(pairs):
            for side, to_refs in enumerate(((keep_near, keep_far), (send_near, send_far))):
                place = lax.bitwise_xor(me, pair * CORES + side) * tokens
                for other in range(near + keep_far.shape[1]):
                    rows = pl.ds(pl.multiple_of(other * own + place, tokens), tokens)
                    to_ref = to_refs[other >= near]
                    to_ref[pair, other % near, :, columns] = out_ref[index, rows, :].astype(to_ref.dtype)


def finish_kernel(
    width, pick, part_count, place_ref, gain_ref, gate, up, s_gate, s_up,
    acc_in, shared_in, square_in, down, s_down, *refs
):
    chunks, refs = refs[:part_count], refs[part_count:]
    (
        hidden_ref, shared_hidden_ref, *outs,
        lhs_ref, square_ref, share_ref, buffer, shared_buffer, s_down_buffer, out_ref, sems,
    ) = refs
    me, node = place_ref[0], place_ref[1]
    late = buffer.shape[0]
    parts = [lax.bitwise_xor(me, part_count - late + index) for index in range(late)]
    moves = weight_moves(parts, (gate, up, s_gate, s_up), (buffer, shared_buffer), sems)
    moves.append(pltpu.make_async_copy(s_down, s_down_buffer, sems.at[len(moves)]))
    queue = Queue(moves)
    experts, inner, shared_inner = gate.shape[0], gate.shape[2], s_gate.shape[1]
    own, depth = shared_in.shape[0], gain_ref.shape[2]
    for index, part in enumerate(parts):
        square_sums(
            chunks[index - late], gain_ref[part], lhs_ref.at[index], square_ref,
            square_ref if index else square_in,
        )
    blocks = row_blocks(chunks[-1].shape[0])
    for rows in blocks:
        tag = sum(chunk[rows, depth:].astype(jnp.float32) for chunk in chunks)
        for expert in range(experts):
            share = row_share(tag, node, pick, experts, expert)
            share_ref[expert, rows, :] = jnp.broadcast_to(share, (share.shape[0], LANES))
        square_ref[rows, :] = lax.rsqrt(square_ref[rows, :] / width + 1e-06)

    def project(rows_list, before, weights):
        terms = [before[rows] for rows in rows_list]
        for index in range(late):
            queue.wait()
            for at, rows in enumerate(rows_list):
                terms[at] = terms[at] + jnp.dot(
                    lhs_ref[index, rows, :], weights(index), preferred_element_type=jnp.float32
                )
        return [term * square_ref[rows, :][:, :1] for term, rows in zip(terms, rows_list)]

    class Columns:
        def __init__(self, ref, start, count):
            self.ref, self.columns = ref, slice(start, start + count)

        def __getitem__(self, rows):
            return self.ref[rows, self.columns]

    projs = []
    for which in range(2):
        before = Columns(shared_in, which * shared_inner, shared_inner)
        projs += project([slice(0, own)], before, lambda index: shared_buffer[index, which])
    shared_hidden_ref[...] = act(*projs).astype(jnp.bfloat16)
    for expert in range(experts):
        projs = []
        for slot in (2 * expert, 2 * expert + 1):
            before = Columns(acc_in, slot * inner, inner)
            projs.append(project(blocks, before, lambda index: buffer[index, slot]))
        for rows, gate_proj, up_proj in zip(blocks, *projs):
            hidden_ref[rows, expert * inner : (expert + 1) * inner] = (
                act(gate_proj, up_proj) * share_ref[expert, rows, :][:, :1]
            ).astype(jnp.bfloat16)
        if expert < experts - 1:
            down_expert(hidden_ref, expert, 0, down, out_ref, range(out_ref.shape[0]))
    queue.wait()
    for index in range(out_ref.shape[0]):
        down_expert(hidden_ref, experts - 1, 0, down, out_ref, [index])
        down_shared(shared_hidden_ref, 0, s_down_buffer, out_ref, [index])
        leave(me, own, out_ref, outs, [index])


def down_kernel(first, place_ref, hidden_ref, shared_hidden_ref, down, s_down, *refs):
    for expert in range(down.shape[0]):
        down_expert(hidden_ref, expert, first, down, refs[-1], range(refs[-1].shape[0]))
    down_shared(shared_hidden_ref, first, s_down, refs[-1], range(refs[-1].shape[0]))
    leave(place_ref[0], shared_hidden_ref.shape[0], refs[-1], refs[:4], range(refs[-1].shape[0]))


def call(kernel, name, out_shape, in_specs, scratch, args, flops=0, read=0, aliases=None):
    held = [a for a, spec in zip(args, in_specs) if spec is VMEM and a.ndim < 3] + list(out_shape)
    held += [s for s in scratch if hasattr(s, "dtype") and s.memory_space == pltpu.VMEM]
    size = 0
    for array in held:
        count = jnp.dtype(array.dtype).itemsize
        for extent in array.shape:
            count *= extent
        size += count
    return pl.pallas_call(
        kernel,
        out_shape=out_shape,
        in_specs=in_specs,
        out_specs=[VMEM] * len(out_shape),
        scratch_shapes=scratch,
        input_output_aliases=aliases or {},
        compiler_params=pltpu.CompilerParams(vmem_limit_bytes=size + 8 * 2**20),
        cost_estimate=pl.CostEstimate(flops=flops, bytes_accessed=read, transcendentals=0),
        name=name,
    )(*args)


def on_device(attended, norm_gain, node_ids, gates, w_gate, w_up, w_down, s_gate, s_up, s_down):
    node_count = lax.axis_size("node")
    local_count = lax.axis_size("local")
    pairs = local_count // CORES
    node, me = lax.axis_index("node"), lax.axis_index("local")
    own, depth = attended.shape
    tokens, pick = node_ids.shape
    experts, width, inner = w_gate.shape
    shared_inner = s_gate.shape[1]
    total = node_count * own
    up_weights = tuple(in_hbm(w) for w in (w_gate, w_up, s_gate, s_up))
    down_weights = (w_down, s_down)
    f32, bf16 = jnp.float32, jnp.bfloat16

    inputs = (
        in_hbm(attended),
        in_hbm(node_ids.T),
        in_hbm(gates.transpose(1, 2, 0).reshape(pick * experts, tokens)),
        in_hbm(norm_gain.reshape(local_count, 1, depth)),
    )
    block, gain = call(
        functools.partial(pack_kernel, pick, experts),
        "pack",
        [
            jax.ShapeDtypeStruct((own, depth + LANES), bf16),
            jax.ShapeDtypeStruct((local_count, 1, depth), f32),
        ],
        [SMEM] + [HBM] * 4,
        [pltpu.VMEM(x.shape, x.dtype) for x in inputs[:3]] + [pltpu.SemaphoreType.DMA((4,))],
        (me[None], *inputs),
        flops=4 * 10**10,
    )
    blocks = [block] + [swap(block, "node", k) for k in range(1, node_count)]
    rest = jnp.concatenate(blocks[1:], axis=0)
    column = jnp.concatenate([block, rest], axis=0)
    chunks = [column, swap(column, "local", 1)]

    def neighbour(k, sums):
        (column,) = call(
            functools.partial(join_kernel, 2),
            "join",
            [jax.ShapeDtypeStruct(chunks[0].shape, bf16)],
            [VMEM, VMEM, ANY],
            [],
            (first_rows[k - 1], other_rows[k - 1], sums[2]),
        )
        return [column, swap(column, "local", 1)]

    first_rows = [swap(block, "local", k * CORES) for k in range(1, pairs)]
    other_rows = [swap(rest, "local", k * CORES) for k in range(1, pairs)]

    sums_shape = [
        jax.ShapeDtypeStruct((total, experts * 2 * inner), f32),
        jax.ShapeDtypeStruct((own, 2 * shared_inner), f32),
        jax.ShapeDtypeStruct((total, LANES), f32),
    ]
    flops = 2 * depth * (total * experts * 2 * inner + own * 2 * shared_inner)
    read = 2 * depth * (experts * 2 * inner + 2 * shared_inner)
    weight_scratch = [
        pltpu.VMEM((1, experts * 2, depth, inner), bf16),
        pltpu.VMEM((1, 2, depth, shared_inner), bf16),
    ]
    lhs_scratch = pltpu.VMEM((total, depth), bf16)
    moves = experts * 2 + 2
    sums = None
    for offset in range(local_count - LATE):
        first = sums is None
        if offset == CORES - 1:
            for k in range(1, pairs):
                chunks += neighbour(k, sums)
        args = (lax.bitwise_xor(me, offset)[None], chunks[offset], gain, *up_weights)
        more = tuple(first_rows) if first else tuple(sums)
        sums = call(
            functools.partial(project_kernel, first, len(more) if first else 0),
            "project",
            sums_shape,
            [SMEM, VMEM, VMEM] + [HBM] * 4 + [ANY if first else VMEM] * len(more),
            [lhs_scratch, *weight_scratch, pltpu.SemaphoreType.DMA((moves,))],
            args + more,
            flops,
            read,
            aliases={} if first else {7: 0, 8: 1, 9: 2},
        )
    place = jnp.stack([me, node])

    slices = max(1, total // ROWS)
    step = width // slices
    half = node_count // 2
    out_shape = [
        jax.ShapeDtypeStruct((pairs, half, tokens, step), dtype)
        for dtype in (f32, f32, bf16, bf16)
    ]
    pieces = max(1, step // (10 * LANES))
    down_scratch = [
        pltpu.VMEM((pieces, total, step // pieces), f32),
    ]
    down_flops = 2 * step * (total * experts * inner + own * shared_inner)
    down_read = 2 * step * (experts * inner + shared_inner)
    partials = []
    for index in range(slices):
        if index == 0:
            hidden, shared_hidden, *out = call(
                functools.partial(finish_kernel, width, pick, local_count),
                "finish",
                [
                    jax.ShapeDtypeStruct((total, experts * inner), bf16),
                    jax.ShapeDtypeStruct((own, shared_inner), bf16),
                ]
                + out_shape,
                [SMEM, VMEM] + [HBM] * 4 + [VMEM] * 4 + [HBM] + [VMEM] * local_count,
                [
                    pltpu.VMEM((LATE, total, depth), bf16),
                    pltpu.VMEM((total, LANES), f32),
                    pltpu.VMEM((experts, total, LANES), f32),
                    *(pltpu.VMEM((LATE, *w.shape[1:]), bf16) for w in weight_scratch),
                    pltpu.VMEM(s_down.shape, bf16),
                    *down_scratch,
                    pltpu.SemaphoreType.DMA((LATE * moves + 1,)),
                ],
                (place, gain, *up_weights, *sums, w_down, in_hbm(s_down), *chunks),
                flops + down_flops,
                read + down_read,
            )
        else:
            out = call(
                functools.partial(down_kernel, index * step),
                "down",
                out_shape,
                [SMEM] + [VMEM] * 4,
                down_scratch,
                (place, hidden, shared_hidden, *down_weights),
                down_flops,
                down_read,
            )
        partials.append(out)

    results = []
    for keep_far, keep_near, send_far, send_near in partials:
        far = keep_far + swap(send_far, "local", 1).astype(f32)
        came = [swap(far[k].astype(bf16), "local", k * CORES) for k in range(1, pairs)]
        near = keep_near + swap(send_near, "local", 1).astype(f32)
        near_came = [
            swap(near[k].astype(bf16), "local", k * CORES).astype(f32) for k in range(1, pairs)
        ]
        far_rows = call(
            relay_kernel,
            "relay",
            [jax.ShapeDtypeStruct((tokens, step), bf16)] * (node_count - half),
            [VMEM] * pairs,
            [],
            (far, *came),
        )
        far_came = [swap(x, "node", half + k).astype(f32) for k, x in enumerate(far_rows)]
        result = sum(near_came, near[0])
        total_here = result[0]
        for k in range(1, half):
            total_here = total_here + swap(result[k].astype(bf16), "node", k).astype(f32)
        total_here = sum(far_came, total_here)
        results.append(total_here)
    mixed = jnp.concatenate(results, axis=1)

    rows = jnp.stack(
        [lax.dynamic_slice(c, (me * tokens, 0), (tokens, depth)) for c in chunks]
    )
    bit = 1
    while bit < local_count:
        flipped = rows.reshape(local_count // (2 * bit), 2, bit, tokens, depth)[:, ::-1]
        rows = jnp.where((me & bit) != 0, flipped.reshape(rows.shape), rows)
        bit *= 2
    residual = rows.transpose(1, 0, 2).reshape(tokens, width).astype(jnp.float32)
    return (residual + mixed).astype(jnp.bfloat16)


def solution(mesh):
    in_specs = (
        P(("group", "node"), "local"),
        P(),
        P(("group", "node", "local"), None),
        P(("group", "node", "local"), None, None),
        P("node", None, "local"),
        P("node", None, "local"),
        P("node", "local", None),
        P(None, "local"),
        P(None, "local"),
        P("local", None),
    )
    out_specs = P(("group", "node", "local"), None)
    return jax.shard_map(
        on_device, mesh=mesh, in_specs=in_specs, out_specs=out_specs, check_vma=False
    )
```
